32 devices in a mesh: dp: 8 (over y, x, core), tensor: 4 (over z).
Axes of the slice: x: 2, y: 2, z: 4, core: 2. Of those that a mesh axis runs over, the one named last changes fastest.
Arguments:
- tokens: bfloat16 [8192, 2048], P(('dp', 'tensor')), may hold values from -6 to 6
- positions: int32 [8192], P(('dp', 'tensor')), may hold values from 0 to 2046, as said below
- attn_gain: float32 [2048], replicated, may hold values from 0.25 to 1.75
- query_weight: bfloat16 [2048, 2048], P('dp', 'tensor'), may hold values from -0.125 to 0.125
- key_weight: bfloat16 [2048, 1024], P('dp', 'tensor'), may hold values from -0.125 to 0.125
- value_weight: bfloat16 [2048, 1024], P('dp', 'tensor'), may hold values from -0.125 to 0.125
- query_gain: float32 [128], replicated, may hold values from 0.25 to 1.75
- key_gain: float32 [128], replicated, may hold values from 0.25 to 1.75
- out_weight: bfloat16 [2048, 2048], P('tensor', 'dp'), may hold values from -1 to 1
- mlp_gain: float32 [2048], replicated, may hold values from 0.25 to 1.75
- gate_weight: bfloat16 [2048, 6144], P('dp', 'tensor'), may hold values from -0.125 to 0.125
- up_weight: bfloat16 [2048, 6144], P('dp', 'tensor'), may hold values from -0.125 to 0.125
- down_weight: bfloat16 [6144, 2048], P('tensor', 'dp'), may hold values from -0.078125 to 0.078125
- cotangent: bfloat16 [8192, 2048], P(('dp', 'tensor')), may hold values from -6 to 6
Outputs:
- mixed: bfloat16 [8192, 2048], P(('dp', 'tensor'))
- token_grad: bfloat16 [8192, 2048], P(('dp', 'tensor'))
- attn_gain_grad: float32 [2048], replicated
- query_weight_grad: float32 [2048, 2048], P('dp', 'tensor')
- key_weight_grad: float32 [2048, 1024], P('dp', 'tensor')
- value_weight_grad: float32 [2048, 1024], P('dp', 'tensor')
- query_gain_grad: float32 [128], replicated
- key_gain_grad: float32 [128], replicated
- out_weight_grad: float32 [2048, 2048], P('tensor', 'dp')
- mlp_gain_grad: float32 [2048], replicated
- gate_weight_grad: float32 [2048, 6144], P('dp', 'tensor')
- up_weight_grad: float32 [2048, 6144], P('dp', 'tensor')
- down_weight_grad: float32 [6144, 2048], P('tensor', 'dp')
The draws below stay inside these ranges and needn't reach their ends.
Inputs may be any that keep to these rules, and one draw needn't show every extreme that they name: `positions`: within each sequence of 1024 consecutive tokens the ids start at 0 and rise by 1 or 2 from one token to the next; in one sequence, drawn from the seed, every rise is 2.
All inputs are finite; a program needn't handle non-finite values.
Results may differ from the reference program's by a relative error of at most 0.02.
Values may be sent and summed in bfloat16 or wider, within the bound.
No kernel may reach another device: no remote copies, remote signals or barrier semaphores. Data moves between devices by JAX's collectives and lax.ppermute only.
A program may use at most 256 MiB of HBM per device.

```python
import jax
import jax.numpy as jnp
from jax import lax

D = 2048
H = 16
KV = 8
HD = 128
FF = 6144
LEN = 1024
TOKENS = 8192


def draw_positions(key, part):
    key = jax.random.fold_in(key, 7)
    seq_total = TOKENS // LEN
    steps = jax.random.randint(key, (seq_total, LEN), 1, 3)
    chosen = jax.random.randint(jax.random.fold_in(key, 11), (), 0, seq_total)
    rows = lax.broadcasted_iota(jnp.int32, (seq_total, LEN), 0)
    steps = jnp.where(rows == chosen, 2, steps)
    leading = lax.broadcasted_iota(jnp.int32, (seq_total, LEN), 1) == 0
    steps = jnp.where(leading, 0, steps)
    return jnp.cumsum(steps, axis=1).reshape(TOKENS).astype(jnp.int32)


def block_scale(key, extent, shards, low, top_value):
    def one(dim, parts):
        draws = jax.random.uniform(jax.random.fold_in(jax.random.fold_in(key, 6), dim), (parts,), jnp.float32, low / len(shards), top_value / len(shards))
        return jnp.repeat(jnp.exp(draws), extent[dim] // parts).reshape((-1,) + (1,) * (len(extent) - dim - 1))

    loudness = one(*shards[0])
    for cut in shards[1:]:
        loudness = loudness * one(*cut)
    return loudness


def bell_draw(stream_key, extent, scale, reach, split=(), kind=jnp.bfloat16):
    values = jax.random.normal(stream_key, extent, jnp.float32) * scale
    if len(split) > 0:
        values = block_scale(stream_key, extent, split, -0.22, 0.18) * values
    return jnp.clip(values, min=-reach, max=reach).astype(kind)


def setup_inputs(seed: int = 0) -> dict:
    key_list = jax.random.split(jax.random.key(seed), 15)
    return {
        "tokens": bell_draw(key_list[0], (TOKENS, D), 1.0, 6.0, ((0, 32),)),
        "positions": draw_positions(jax.random.fold_in(key_list[14], 71), 0),
        "attn_gain": jnp.clip(1.0 + 0.15 * jax.random.normal(key_list[2], (D,), jnp.float32), 0.25, 1.75),
        "query_weight": bell_draw(key_list[3], (D, H * HD), D ** -0.5, 0.125, ((0, 8), (1, 4))),
        "key_weight": bell_draw(key_list[4], (D, KV * HD), D ** -0.5, 0.125, ((0, 8), (1, 4))),
        "value_weight": bell_draw(key_list[5], (D, KV * HD), D ** -0.5, 0.125, ((0, 8), (1, 4))),
        "query_gain": jnp.clip(1.0 + 0.15 * jax.random.normal(key_list[6], (HD,), jnp.float32), 0.25, 1.75),
        "key_gain": jnp.clip(1.0 + 0.15 * jax.random.normal(key_list[7], (HD,), jnp.float32), 0.25, 1.75),
        "out_weight": bell_draw(key_list[8], (H * HD, D), (H * HD // 64) ** -0.5, 1.0, ((0, 4), (1, 8))),
        "mlp_gain": jnp.clip(1.0 + 0.15 * jax.random.normal(key_list[9], (D,), jnp.float32), 0.25, 1.75),
        "gate_weight": bell_draw(key_list[10], (D, FF), D ** -0.5, 0.125, ((0, 8), (1, 4))),
        "up_weight": bell_draw(key_list[11], (D, FF), D ** -0.5, 0.125, ((0, 8), (1, 4))),
        "down_weight": bell_draw(key_list[12], (FF, D), FF ** -0.5, 0.078125, ((0, 4), (1, 8))),
        "cotangent": bell_draw(key_list[13], (TOKENS, D), 1.0, 6.0, ((0, 32),)),
    }


@jax.custom_vjp
def low(v):
    return lax.optimization_barrier(v.astype(jnp.bfloat16)).astype(jnp.float32)

@jax.custom_vjp
def low_back(v):
    return v

def low_keep(v):
    return (low(v), None)

def low_pass(kept, grad):
    return (grad,)

def back_keep(v):
    return (v, None)

def back_low(kept, grad):
    return (low(grad),)
low.defvjp(low_keep, low_pass)
low_back.defvjp(back_keep, back_low)
EPSILON = 1e-06
NEGATIVE = -1e+30

def rms_scale(vector, gains):
    return vector * lax.rsqrt(lax.optimization_barrier(jnp.mean(vector * vector, axis=-1, keepdims=True)) + EPSILON) * gains

def turn_half(vector):
    half_width = vector.shape[-1] // 2
    return jnp.concatenate([-vector[..., half_width:], vector[..., :half_width]], axis=-1)

def rotate(vector, cosine, sine_table):
    return vector * cosine + turn_half(vector) * sine_table

def angle_tables(places, width):
    frequency = 1000000.0 ** (-jnp.arange(0, width, 2, dtype=jnp.float32) / width)
    angles = places.astype(jnp.float32)[:, None] * frequency[None, :]
    angles = jnp.concatenate([angles, angles], axis=-1)
    return (jnp.cos(angles), jnp.sin(angles))

def matmul_high(left, right):
    return jnp.dot(left, right, precision=lax.Precision.HIGHEST, preferred_element_type=jnp.float32)

def layer_forward(sequence, cosine, sine_table, attn_gain, query_weight, key_weight, value_weight, query_gain, key_gain, out_weight, mlp_gain, gate_weight, up_weight, down_weight):
    length = sequence.shape[0]
    normed = low(rms_scale(sequence, attn_gain))
    q_proj = low_back(matmul_high(normed, query_weight)).reshape(length, H, HD)
    k_proj = low_back(matmul_high(normed, key_weight)).reshape(length, KV, HD)
    v_proj = low_back(matmul_high(normed, value_weight)).reshape(length, KV, HD)
    queries = low(rotate(rms_scale(q_proj, query_gain), cosine[:, None], sine_table[:, None]))
    keys = low(rotate(rms_scale(k_proj, key_gain), cosine[:, None], sine_table[:, None]))
    values = low(v_proj)
    keys = jnp.repeat(keys, H // KV, axis=1)
    values = jnp.repeat(values, H // KV, axis=1)
    raw_scores = jnp.einsum('qhd,khd->hqk', queries, keys, precision=lax.Precision.HIGHEST)
    scores = low_back(raw_scores * HD ** (-0.5))
    allowed = jnp.arange(length)[:, None] >= jnp.arange(length)[None, :]
    scores = jnp.where(allowed[None], scores, NEGATIVE)
    probs = jax.nn.softmax(scores, axis=-1)
    attended = jnp.einsum('hqk,khd->qhd', low(probs), values, precision=lax.Precision.HIGHEST)
    attended = low(low_back(attended)).reshape(length, H * HD)
    hidden_rows = sequence + low_back(matmul_high(attended, out_weight))
    mlp_in = low(rms_scale(hidden_rows, mlp_gain))
    gate_act = low_back(matmul_high(mlp_in, gate_weight))
    up_act = low_back(matmul_high(mlp_in, up_weight))
    hidden = low(jax.nn.silu(gate_act) * up_act)
    return hidden_rows + matmul_high(hidden, down_weight)

def reference(tokens, positions, attn_gain, query_weight, key_weight, value_weight, query_gain, key_gain, out_weight, mlp_gain, gate_weight, up_weight, down_weight, cotangent):
    seq_count = tokens.shape[0] // LEN
    cosine, sine_table = angle_tables(positions, HD)
    cosine = cosine.reshape(seq_count, LEN, HD)
    sine_table = sine_table.reshape(seq_count, LEN, HD)
    parameters = tuple((weight.astype(jnp.float32) for weight in (attn_gain, query_weight, key_weight, value_weight, query_gain, key_gain, out_weight, mlp_gain, gate_weight, up_weight, down_weight)))

    def forward(inputs, weights_all):

        def per_sequence(pieces):
            return jax.checkpoint(layer_forward)(pieces[0], pieces[1], pieces[2], *weights_all)
        stacked = lax.map(per_sequence, (inputs.reshape(seq_count, LEN, -1), cosine, sine_table))
        return stacked.reshape(inputs.shape)
    result, pull_back = jax.vjp(forward, tokens.astype(jnp.float32), parameters)
    input_grad, gradients = pull_back(cotangent.astype(jnp.float32))
    return (result.astype(jnp.bfloat16), input_grad.astype(jnp.bfloat16), gradients[0], gradients[1], gradients[2], gradients[3], gradients[4], gradients[5], gradients[6], gradients[7], gradients[8], gradients[9], gradients[10])
```

```python
import jax
import jax.numpy as jnp
from jax import lax
from jax.experimental import pallas as pl
from jax.experimental.pallas import tpu as pltpu
from jax.sharding import PartitionSpec as P

HD = 128
LEN = 1024

EPSILON = 1e-06
NEGATIVE = -1e30

f32 = jnp.float32
bf16 = jnp.bfloat16


def rms_norm(vector):
    scale = lax.rsqrt(jnp.mean(vector * vector, axis=-1, keepdims=True) + EPSILON)
    return vector * scale, scale


def rms_back(grad, gains, normal, scale):
    weighted = grad * gains
    return scale * (weighted - normal * jnp.mean(weighted * normal, axis=-1, keepdims=True))


def angle_tables(places, width):
    frequency = 1000000.0 ** (-jnp.arange(0, width, 2, dtype=f32) / width)
    angles = places.astype(f32)[:, None] * frequency[None, :]
    cosine, sine = jnp.cos(angles), jnp.sin(angles)
    return (
        jnp.concatenate([cosine, cosine], axis=-1),
        jnp.concatenate([-sine, sine], axis=-1),
    )


def contract(left, right, left_dim, right_dim):
    return lax.dot_general(
        left, right, (((left_dim,), (right_dim,)), ((), ())), preferred_element_type=f32
    )


def fence(*trees):
    leaves, shape = jax.tree.flatten(trees)
    return jax.tree.unflatten(shape, lax.optimization_barrier(leaves))


def after(value, *others):
    return fence(value, others)[0]


def pass_on(value, axis):
    count = lax.axis_size(axis)
    return lax.ppermute(value, axis, [(i, (i + 1) % count) for i in range(count)])


class Halving:
    def __init__(self, blocks, axis):
        self.axis, self.count = axis, lax.axis_size(axis)
        self.bits = self.count.bit_length() - 1
        assert self.count == 1 << self.bits
        rows = blocks.shape[0] // self.count
        blocks = blocks.reshape((2,) * self.bits + (rows,) + blocks.shape[1:])
        self.halves = tuple(jnp.split(blocks, 2, axis=self.bits + 1))
        others = list(range(1, self.bits))
        self.orders = ([0] + others, [0] + others[::-1])
        self.left = [list(range(self.bits))[::-1], list(range(self.bits))[::-1]]
        self.steps = 0

    def step(self):
        place = lax.axis_index(self.axis)
        done = []
        for half, order, left in zip(self.halves, self.orders, self.left):
            bit = order[self.steps]
            dim = left.index(bit)
            mine = lax.rem(lax.div(place, 1 << bit), 2)
            keep = lax.dynamic_index_in_dim(half, mine, dim, keepdims=False)
            send = lax.dynamic_index_in_dim(half, 1 - mine, dim, keepdims=False)
            pairs = [(i, i ^ (1 << bit)) for i in range(self.count)]
            done.append(keep + lax.ppermute(send, self.axis, pairs))
            left.remove(bit)
        self.halves = tuple(done)
        self.steps += 1
        return self

    @property
    def state(self):
        return self.halves

    @state.setter
    def state(self, value):
        self.halves = value

    def total(self):
        while self.steps < self.bits:
            self.step()
        return jnp.concatenate(self.halves, axis=1)


def butterfly_sum(value, axis):
    count = lax.axis_size(axis)
    if count & (count - 1):
        return lax.psum(value, axis)
    bit = 1
    while bit < count:
        value = value + lax.ppermute(value, axis, [(i, i ^ bit) for i in range(count)])
        bit *= 2
    return value


def rows_of(array, index, rows):
    return lax.dynamic_slice_in_dim(array, index * rows, rows, axis=0)


def in_order(blocks, axis, sign, dim=0):
    count = lax.axis_size(axis)
    place = lax.axis_index(axis)
    size = blocks[0].shape[dim]
    shape = list(blocks[0].shape)
    shape[dim] *= count
    whole = jnp.zeros(shape, blocks[0].dtype)
    for step, block in enumerate(blocks):
        owner = lax.rem(place + sign * step + count, count)
        whole = lax.dynamic_update_slice_in_dim(whole, block, owner * size, axis=dim)
    return whole


VMEM_LIMIT = 48 * 2**20
QUERY_ROWS = 256


def dot(left, right, left_dim=1, right_dim=0):
    return contract(left, right, left_dim, right_dim)


def project_kernel(q_blocks, k_blocks, _, rows, weight, cosine, sine, gains, __, ___, out, saved):
    block = pl.program_id(0)
    projected = dot(rows[...], weight[...])

    @pl.when(block < q_blocks + k_blocks)
    def _():
        saved[...] = projected
        gain = jnp.where(block < q_blocks, gains[0:1], gains[1:2])
        for first in range(0, projected.shape[1], HD):
            normal = rms_norm(projected[:, first : first + HD])[0] * gain
            turned = pltpu.roll(normal, HD // 2, 1) * sine[...]
            out[:, first : first + HD] = (normal * cosine[...] + turned).astype(bf16)

    @pl.when(block >= q_blocks + k_blocks)
    def _():
        out[...] = projected.astype(bf16)


def project(owner, rows, own_rows, weight, cosine, sine, gains, out, saved, q_cols, k_cols):
    depth, columns = weight.shape
    step = min(k_cols, 256)
    q_blocks, k_blocks = q_cols // step, k_cols // step
    grid = columns // step
    whole = lambda j, o: (0, 0)
    return pl.pallas_call(
        lambda *refs: project_kernel(q_blocks, k_blocks, *refs),
        out_shape=(
            jax.ShapeDtypeStruct(out.shape, out.dtype),
            jax.ShapeDtypeStruct(saved.shape, saved.dtype),
        ),
        grid_spec=pltpu.PrefetchScalarGridSpec(
            num_scalar_prefetch=1,
            grid=(grid,),
            in_specs=[
                pl.BlockSpec((own_rows, depth), whole),
                pl.BlockSpec((depth, step), lambda j, o: (0, j)),
                pl.BlockSpec((own_rows, HD), whole),
                pl.BlockSpec((own_rows, HD), whole),
                pl.BlockSpec((2, HD), whole),
                pl.BlockSpec(memory_space=pl.ANY),
                pl.BlockSpec(memory_space=pl.ANY),
            ],
            out_specs=(
                pl.BlockSpec((own_rows, step), lambda j, o: (o[0], j)),
                pl.BlockSpec(
                    (own_rows, step),
                    lambda j, o: (o[0], jnp.minimum(j, q_blocks + k_blocks - 1)),
                ),
            ),
        ),
        input_output_aliases={6: 0, 7: 1},
        compiler_params=pltpu.CompilerParams(vmem_limit_bytes=VMEM_LIMIT),
        cost_estimate=pl.CostEstimate(
            flops=2 * own_rows * depth * columns,
            bytes_accessed=2 * depth * (own_rows + columns) + 6 * own_rows * columns,
            transcendentals=0,
        ),
    )(owner, rows, weight, cosine, sine, gains, out, saved)


def masked_scores(query, key, first):
    scores = dot(query, key, 1, 1) * (HD ** (-0.5))
    row = lax.broadcasted_iota(jnp.int32, scores.shape, 0) + first
    return jnp.where(row >= lax.broadcasted_iota(jnp.int32, scores.shape, 1), scores, NEGATIVE)


def softmax(scores):
    exponent = jnp.exp(scores - jnp.max(scores, axis=1, keepdims=True))
    return exponent * (1.0 / jnp.sum(exponent, axis=1, keepdims=True))


def attend_kernel(queries, keys, values, out):
    rows = min(QUERY_ROWS, queries.shape[0])
    for first in range(0, queries.shape[0], rows):
        last = first + rows
        for head in range(0, queries.shape[1], HD):
            probs = softmax(
                masked_scores(queries[first:last, head : head + HD], keys[:last], first)
            )
            out[first:last, head : head + HD] = dot(probs.astype(bf16), values[:last]).astype(bf16)


def attend(qkv, length, q_cols, k_cols):
    rows = qkv.shape[0]
    groups = k_cols // HD
    share = q_cols // groups
    return pl.pallas_call(
        attend_kernel,
        out_shape=jax.ShapeDtypeStruct((rows, q_cols), bf16),
        grid=(rows // length, groups),
        in_specs=[
            pl.BlockSpec((length, share), lambda s, g: (s, g)),
            pl.BlockSpec((length, HD), lambda s, g: (s, q_cols // HD + g)),
            pl.BlockSpec((length, HD), lambda s, g: (s, (q_cols + k_cols) // HD + g)),
        ],
        out_specs=pl.BlockSpec((length, share), lambda s, g: (s, g)),
        compiler_params=pltpu.CompilerParams(vmem_limit_bytes=VMEM_LIMIT),
        cost_estimate=pl.CostEstimate(
            flops=4 * rows * length * q_cols,
            bytes_accessed=2 * rows * (2 * q_cols + 2 * k_cols),
            transcendentals=rows * length * q_cols // HD,
        ),
    )(qkv, qkv, qkv)


def unrope_unnorm(grad, projected, gain, cosine, sine):
    grad = grad * cosine + pltpu.roll(grad * sine, HD // 2, 1)
    normal, scale = rms_norm(projected)
    return rms_back(grad, gain, normal, scale), grad * normal


def attend_back_kernel(
    queries, keys, values, grads, q_proj, k_proj, cosine, sine, gains,
    q_out, k_out, v_out, gain_out, key_grad, value_grad,
):
    length = queries.shape[0]
    rows = min(QUERY_ROWS, length)
    scale = HD ** (-0.5)
    gain_total = jnp.zeros((1, HD), f32)
    for first in range(length - rows, -1, -rows):
        last = first + rows
        for head in range(0, queries.shape[1], HD):
            columns = slice(head, head + HD)
            query, grad = queries[first:last, columns], grads[first:last, columns]
            probs = softmax(masked_scores(query, keys[:last], first))
            prob_grad = dot(grad, values[:last], 1, 1)
            delta = jnp.sum(probs * prob_grad, axis=1, keepdims=True)
            score_grad = (probs * (prob_grad - delta)).astype(bf16)
            value_part = dot(probs.astype(bf16), grad, 0, 0)
            key_part = dot(score_grad, query, 0, 0)
            if last == length and head == 0:
                key_grad[...] = key_part
                value_grad[...] = value_part
            else:
                key_grad[:last] += key_part
                value_grad[:last] += value_part
            out, gain_rows = unrope_unnorm(
                dot(score_grad, keys[:last]) * scale,
                q_proj[first:last, columns],
                gains[0:1],
                cosine[first:last],
                sine[first:last],
            )
            q_out[first:last, columns] = out.astype(bf16)
            gain_total += jnp.sum(gain_rows, axis=0, keepdims=True)
    out, gain_rows = unrope_unnorm(
        key_grad[...] * scale, k_proj[...], gains[1:2], cosine[...], sine[...]
    )
    k_out[...] = out.astype(bf16)
    v_out[...] = value_grad[...].astype(bf16)
    gain_out[0, 0:1] = gain_total
    gain_out[0, 1:2] = jnp.sum(gain_rows, axis=0, keepdims=True)


def attend_back(qkv, grads, saved, cosine, sine, gains, length, q_cols, k_cols):
    rows = qkv.shape[0]
    groups = k_cols // HD
    share = q_cols // groups
    return pl.pallas_call(
        attend_back_kernel,
        out_shape=(
            jax.ShapeDtypeStruct((rows, q_cols), bf16),
            jax.ShapeDtypeStruct((rows, k_cols), bf16),
            jax.ShapeDtypeStruct((rows, k_cols), bf16),
            jax.ShapeDtypeStruct((rows // length * groups, 2, HD), f32),
        ),
        grid=(rows // length, groups),
        in_specs=[
            pl.BlockSpec((length, share), lambda s, g: (s, g)),
            pl.BlockSpec((length, HD), lambda s, g: (s, q_cols // HD + g)),
            pl.BlockSpec((length, HD), lambda s, g: (s, (q_cols + k_cols) // HD + g)),
            pl.BlockSpec((length, share), lambda s, g: (s, g)),
            pl.BlockSpec((length, share), lambda s, g: (s, g)),
            pl.BlockSpec((length, HD), lambda s, g: (s, q_cols // HD + g)),
            pl.BlockSpec((length, HD), lambda s, g: (s, 0)),
            pl.BlockSpec((length, HD), lambda s, g: (s, 0)),
            pl.BlockSpec((2, HD), lambda s, g: (0, 0)),
        ],
        out_specs=(
            pl.BlockSpec((length, share), lambda s, g: (s, g)),
            pl.BlockSpec((length, HD), lambda s, g: (s, g)),
            pl.BlockSpec((length, HD), lambda s, g: (s, g)),
            pl.BlockSpec((1, 2, HD), lambda s, g: (s * groups + g, 0, 0)),
        ),
        scratch_shapes=[pltpu.VMEM((length, HD), f32), pltpu.VMEM((length, HD), f32)],
        compiler_params=pltpu.CompilerParams(vmem_limit_bytes=VMEM_LIMIT),
        cost_estimate=pl.CostEstimate(
            flops=8 * rows * length * q_cols,
            bytes_accessed=rows * (10 * q_cols + 12 * k_cols),
            transcendentals=rows * length * q_cols // HD,
        ),
    )(qkv, qkv, qkv, grads, saved, saved, cosine, sine, gains)


def per_device(
    tokens,
    positions,
    attn_gain,
    query_weight,
    key_weight,
    value_weight,
    query_gain,
    key_gain,
    out_weight,
    mlp_gain,
    gate_weight,
    up_weight,
    down_weight,
    cotangent,
):
    own_rows, width = tokens.shape
    count = lax.axis_size("tensor")
    place = lax.axis_index("tensor")
    length = LEN
    q_cols, k_cols = query_weight.shape[1], key_weight.shape[1]
    head_cols = out_weight.shape[0]
    units = gate_weight.shape[1]

    def cut(rows, part):
        return rows[part * own_rows : (part + 1) * own_rows]

    w_out_rows = lax.all_gather(out_weight, "tensor", axis=0, tiled=True)
    w_qkv = lax.all_gather(
        jnp.concatenate([query_weight, key_weight, value_weight], axis=1), "dp", axis=0, tiled=True
    )

    x_rows = tokens.astype(f32)
    x_normal, x_scale = rms_norm(x_rows)
    digits = jnp.stack([positions // 128, positions % 128]).astype(bf16)
    digits = jnp.pad(digits, ((0, 30), (0, width - own_rows)))
    blocks = [jnp.concatenate([(x_normal * attn_gain).astype(bf16), digits], axis=0)]
    gate_up = jnp.concatenate([gate_weight, up_weight], axis=1)
    for step in range(1, count):
        blocks.append(pass_on(blocks[-1], "tensor"))
        if step == 1:
            w_out = lax.all_gather(after(w_out_rows, blocks[-1]), "dp", axis=1, tiled=True)
        if step == min(2, count - 1):
            w_gate_up = lax.all_gather(after(gate_up, blocks[-1]), "dp", axis=0, tiled=True)
    w_down = lax.all_gather(after(down_weight, blocks[-1]), "dp", axis=1, tiled=True)
    cots = [after(cotangent, blocks[-1])]
    cots.append(pass_on(cots[-1], "tensor"))

    group_rows = count * own_rows
    qkv = jnp.zeros((group_rows, q_cols + 2 * k_cols), bf16)
    saved = jnp.zeros((group_rows, q_cols + k_cols), f32)
    head_gains = jnp.stack([query_gain, key_gain])
    tables = []
    for step, block in enumerate(blocks):
        digit_rows = block[own_rows : own_rows + 2, :own_rows].astype(f32)
        tables.append(angle_tables(digit_rows[0] * 128.0 + digit_rows[1], HD))
        qkv, saved = project(
            lax.rem(place - step + count, count).reshape(1),
            block,
            own_rows,
            w_qkv,
            *tables[-1],
            head_gains,
            qkv,
            saved,
            q_cols,
            k_cols,
        )
    cosine = in_order([pair[0] for pair in tables], "tensor", -1)
    sine = in_order([pair[1] for pair in tables], "tensor", -1)
    attended_heads = attend(qkv, length, q_cols, k_cols)

    pieces = [rows_of(attended_heads, place, own_rows)]
    for step in range(1, count):
        piece = rows_of(attended_heads, lax.rem(place + step, count), own_rows)
        pieces.append(lax.ppermute(piece, "tensor", [(i, (i + step) % count) for i in range(count)]))
    pieces, cots[-1] = fence(pieces, cots[-1])
    while len(cots) < count:
        cots.append(pass_on(cots[-1], "tensor"))
    attended = in_order(pieces, "tensor", -1, 1)
    hidden_rows = x_rows + jnp.dot(attended, w_out, preferred_element_type=f32)
    h_normal, h_scale = rms_norm(hidden_rows)

    ins = [(h_normal * mlp_gain).astype(bf16)]
    for step in range(1, count):
        ins.append(pass_on(ins[-1], "tensor"))
    hiddens, grads, parts = [None] * count, [None] * count, [None] * count
    grad_sum = None
    for step in list(range(1, count)) + [0]:
        act = jnp.dot(ins[step], w_gate_up, preferred_element_type=f32)
        gate_act, up_act = act[:, :units], act[:, units:]
        sigmoid = jax.nn.sigmoid(gate_act)
        silu = gate_act * sigmoid
        hiddens[step] = (silu * up_act).astype(bf16)
        hidden_grad = contract(cots[step], w_down, 1, 1)
        gate_grad = hidden_grad * up_act * sigmoid * (1.0 + gate_act * (1.0 - sigmoid))
        grads[step] = jnp.concatenate(
            [gate_grad.astype(bf16), (hidden_grad * silu).astype(bf16)], axis=1
        )
        part = contract(grads[step], w_gate_up, 1, 1)
        if grad_sum is not None:
            part = part + grad_sum.astype(f32)
        if step:
            grad_sum = pass_on(part.astype(bf16), "tensor")
        else:
            mlp_in_grad = part

    all_hidden, all_cot = jnp.concatenate(hiddens, axis=0), jnp.concatenate(cots, axis=0)
    all_in, all_grads = jnp.concatenate(ins, axis=0), jnp.concatenate(grads, axis=0)
    down_wgrad = contract(all_hidden, all_cot, 0, 0).astype(bf16)
    down_sum = lax.psum_scatter(down_wgrad, "dp", scatter_dimension=1, tiled=True)
    gate_up_wgrad = contract(all_in, all_grads, 0, 0).astype(bf16)
    gate_up_sum = lax.psum_scatter(gate_up_wgrad, "dp", scatter_dimension=0, tiled=True)

    rows_grad = cotangent.astype(f32) + rms_back(mlp_in_grad, mlp_gain, h_normal, h_scale)
    mlp_gain_part = jnp.sum(mlp_in_grad * h_normal, axis=0)
    branch_grad = rows_grad.astype(bf16)
    attended_grad = contract(branch_grad, w_out, 1, 1).astype(bf16)

    pieces = []
    for step in range(count):
        first = lax.rem(place - step + count, count) * head_cols
        piece = lax.dynamic_slice_in_dim(attended_grad, first, head_cols, axis=1)
        if step:
            piece = lax.ppermute(piece, "tensor", [(i, (i - step) % count) for i in range(count)])
        pieces.append(piece)
    out_wgrad = contract(branch_grad, attended, 0, 0).astype(bf16)
    out_rows_sum = Halving(out_wgrad, "dp")
    out_part = jnp.dot(hiddens[1 % count], w_down, preferred_element_type=f32)
    pieces, out_rows_sum.state, down_sum, out_part = fence(
        pieces, out_rows_sum.state, down_sum, out_part
    )
    heads_grad = in_order(pieces, "tensor", 1)
    out_rows_sum.step()
    out_rows_sum.step()

    out_grad_sum = pass_on(out_part.astype(bf16), "tensor") if count > 1 else None
    q_grad, k_grad, v_grad, gain_parts = attend_back(
        qkv, heads_grad, saved, cosine, sine, head_gains, length, q_cols, k_cols
    )
    q_grad, k_grad, v_grad, out_rows_sum.state, out_grad_sum = fence(
        q_grad, k_grad, v_grad, out_rows_sum.state, out_grad_sum
    )
    gain_parts = jnp.sum(gain_parts, axis=0)
    proj_grads = [None] * count
    normed_sum = None
    for step in list(range(1, count)) + [0]:
        owner = lax.rem(place - step + count, count)
        proj_grads[step] = jnp.concatenate(
            [rows_of(grad, owner, own_rows) for grad in (q_grad, k_grad, v_grad)], axis=1
        )
        part = contract(proj_grads[step], w_qkv, 1, 1)
        if normed_sum is not None:
            part = part + normed_sum.astype(f32)
        if step:
            normed_sum = pass_on(part.astype(bf16), "tensor")
        else:
            normed_grad = part

    qkv_wgrad = contract(
        jnp.concatenate([block[:own_rows] for block in blocks], axis=0),
        jnp.concatenate(proj_grads, axis=0),
        0,
        0,
    )
    attn_gain_part = jnp.sum(qkv_wgrad * w_qkv.astype(f32), axis=1) / attn_gain
    qkv_sum = Halving(qkv_wgrad.astype(bf16), "dp").step()
    out_rows_sum = out_rows_sum.total().T
    out_blocks = [rows_of(out_rows_sum, lax.rem(place - s + count, count), head_cols) for s in range(count)]
    gains = jnp.concatenate([attn_gain_part, mlp_gain_part, gain_parts.reshape(-1)])
    gains = butterfly_sum(gains.reshape(-1, HD), "dp")
    for step in list(range(2, count)) + [0]:
        out_part = jnp.dot(hiddens[step], w_down, preferred_element_type=f32)
        out_part = out_part + out_grad_sum.astype(f32)
        if step:
            out_grad_sum = pass_on(out_part.astype(bf16), "tensor")
    mixed = (hidden_rows + out_part).astype(bf16)
    out_sum = out_blocks[1 % count]
    for step in list(range(2, count)) + [0]:
        out_sum = pass_on(out_sum, "tensor") + out_blocks[step]
    qkv_sum = qkv_sum.total()
    gains = butterfly_sum(gains, "tensor").reshape(-1)
    token_grad = (rows_grad + rms_back(normed_grad, attn_gain, x_normal, x_scale)).astype(bf16)
    return (
        mixed,
        token_grad,
        gains[:width],
        qkv_sum[:, :q_cols].astype(f32),
        qkv_sum[:, q_cols : q_cols + k_cols].astype(f32),
        qkv_sum[:, q_cols + k_cols :].astype(f32),
        gains[2 * width : 2 * width + HD],
        gains[2 * width + HD :],
        out_sum.astype(f32),
        gains[width : 2 * width],
        gate_up_sum[:, :units].astype(f32),
        gate_up_sum[:, units:].astype(f32),
        down_sum.astype(f32),
    )


def solution(mesh):
    in_specs = (
        P(("dp", "tensor"), None),
        P(("dp", "tensor")),
        P(),
        P("dp", "tensor"),
        P("dp", "tensor"),
        P("dp", "tensor"),
        P(),
        P(),
        P("tensor", "dp"),
        P(),
        P("dp", "tensor"),
        P("dp", "tensor"),
        P("tensor", "dp"),
        P(("dp", "tensor"), None),
    )
    out_specs = (
        P(("dp", "tensor"), None),
        P(("dp", "tensor"), None),
        P(),
        P("dp", "tensor"),
        P("dp", "tensor"),
        P("dp", "tensor"),
        P(),
        P(),
        P("tensor", "dp"),
        P(),
        P("dp", "tensor"),
        P("dp", "tensor"),
        P("tensor", "dp"),
    )
    return jax.shard_map(
        per_device, mesh=mesh, in_specs=in_specs, out_specs=out_specs, check_vma=False
    )
```

```python
import jax
import jax.numpy as jnp
from jax import lax
from jax.experimental import pallas as pl
from jax.experimental.pallas import tpu as pltpu
from jax.sharding import PartitionSpec as P

HD = 128
LEN = 1024

EPSILON = 1e-06
NEGATIVE = -1e30

f32 = jnp.float32
bf16 = jnp.bfloat16


def rms_norm(vector):
    scale = lax.rsqrt(jnp.mean(vector * vector, axis=-1, keepdims=True) + EPSILON)
    return vector * scale, scale


def rms_back(grad, gains, normal, scale):
    weighted = grad * gains
    return scale * (weighted - normal * jnp.mean(weighted * normal, axis=-1, keepdims=True))


def angle_tables(places, width):
    frequency = 1000000.0 ** (-jnp.arange(0, width, 2, dtype=f32) / width)
    angles = places.astype(f32)[:, None] * frequency[None, :]
    cosine, sine = jnp.cos(angles), jnp.sin(angles)
    return (
        jnp.concatenate([cosine, cosine], axis=-1),
        jnp.concatenate([-sine, sine], axis=-1),
    )


def contract(left, right, left_dim, right_dim):
    return lax.dot_general(
        left, right, (((left_dim,), (right_dim,)), ((), ())), preferred_element_type=f32
    )


def fence(*trees):
    leaves, shape = jax.tree.flatten(trees)
    return jax.tree.unflatten(shape, lax.optimization_barrier(leaves))


def after(value, *others):
    return fence(value, others)[0]


def pass_on(value, axis):
    count = lax.axis_size(axis)
    return lax.ppermute(value, axis, [(i, (i + 1) % count) for i in range(count)])


def sum_kernel(count, _, *refs):
    total = refs[0][...].astype(f32)
    for more in refs[1:count]:
        total += more[...].astype(f32)
    refs[count][...] = total.astype(refs[count].dtype)


def sum_blocks(places, arrays, half, rows, dtype):
    size, columns = len(places[0]), arrays[0].shape[2]
    flat = jnp.stack([jnp.asarray(p, jnp.int32) for line in places for p in line])

    def spec(i):
        whole = arrays[i].shape[1] == rows
        return pl.BlockSpec(
            (1, rows, columns), lambda k, at: (at[i * size + k], 0 if whole else half, 0)
        )

    return pl.pallas_call(
        lambda *refs: sum_kernel(len(arrays), *refs),
        out_shape=jax.ShapeDtypeStruct((size, rows, columns), dtype),
        grid_spec=pltpu.PrefetchScalarGridSpec(
            num_scalar_prefetch=1,
            grid=(size,),
            in_specs=[spec(i) for i in range(len(arrays))],
            out_specs=pl.BlockSpec((1, rows, columns), lambda k, at: (k, 0, 0)),
        ),
        compiler_params=pltpu.CompilerParams(vmem_limit_bytes=VMEM_LIMIT),
        cost_estimate=COST,
    )(flat, *arrays)


class HalvingSum:
    def __init__(self, blocks, axis):
        self.axis, self.count = axis, lax.axis_size(axis)
        self.bits = self.count.bit_length() - 1
        assert self.count == 1 << self.bits
        self.rows = blocks.shape[0] // self.count
        others = list(range(1, self.bits))
        self.orders = ([0] + others, [0] + others[::-1])
        self.state = (blocks.reshape((self.count, self.rows) + blocks.shape[1:]), [])
        self.steps = 0

    def mine(self, bit):
        return lax.rem(lax.div(lax.axis_index(self.axis), 1 << bit), 2)

    def addends(self, half, step, sent):
        order = self.orders[half]
        free = sorted(order[step + 1 :]) if sent else []
        blocks = []
        for number in range(1 << len(free)):
            value = {bit: (number >> rank) & 1 for rank, bit in enumerate(free)}
            for bit in order:
                if bit not in value:
                    value[bit] = self.mine(bit)
            if sent:
                value[order[step]] = 1 - value[order[step]]
            blocks.append(value)
        arrays = [(self.state[0], sorted(order))]
        for before, arrived in enumerate(self.state[1]):
            pieces = arrived[min(half, len(arrived) - 1)]
            pieces = pieces[0] if len(pieces) == 1 else jnp.concatenate(pieces, axis=0)
            arrays.append((pieces, sorted(order[before + 1 :])))
        places = [
            [sum((v[bit] << rank for rank, bit in enumerate(bits)), jnp.int32(0)) for v in blocks]
            for _, bits in arrays
        ]
        return places, [array for array, _ in arrays]

    def prepare(self):
        first = self.steps == 0
        self.sends = []
        for half in range(1 if first else 2):
            places, arrays = self.addends(half, self.steps, True)
            rows = self.rows if first else self.rows // 2
            self.sends.append(sum_blocks(places, arrays, half, rows, bf16))
        return self

    def launch(self, piece_size):
        arrived = []
        for half, send in enumerate(self.sends):
            bit = self.orders[half][self.steps]
            pairs = [(i, i ^ (1 << bit)) for i in range(self.count)]
            parts = max(1, send.size // piece_size)
            pieces = jnp.split(send, parts) if send.shape[0] % parts == 0 else [send]
            arrived.append([lax.ppermute(piece, self.axis, pairs) for piece in pieces])
        self.state = (self.state[0], self.state[1] + [arrived])
        self.steps += 1
        return self

    def step(self):
        return self if self.steps == self.bits else self.prepare().launch(self.state[0].size)

    def total(self, dtype):
        while self.steps < self.bits:
            self.step()
        halves = []
        for half in range(2):
            places, arrays = self.addends(half, self.bits, False)
            halves.append(sum_blocks(places, arrays, half, self.rows // 2, dtype)[0])
        return jnp.concatenate(halves, axis=0)


def direct_sum(value, axis):
    count = lax.axis_size(axis)
    total = value
    for step in range(1, count):
        total = total + lax.ppermute(value, axis, [(i, (i + step) % count) for i in range(count)])
    return total


def rows_of(array, index, rows):
    return lax.dynamic_slice_in_dim(array, index * rows, rows, axis=0)


def in_order(blocks, axis, sign, dim=0):
    count = lax.axis_size(axis)
    place = lax.axis_index(axis)
    size = blocks[0].shape[dim]
    shape = list(blocks[0].shape)
    shape[dim] *= count
    whole = jnp.zeros(shape, blocks[0].dtype)
    for step, block in enumerate(blocks):
        owner = lax.rem(place + sign * step + count, count)
        whole = lax.dynamic_update_slice_in_dim(whole, block, owner * size, axis=dim)
    return whole


VMEM_LIMIT = 48 * 2**20
COST = pl.CostEstimate(flops=2**20, bytes_accessed=2**20, transcendentals=0)
QUERY_ROWS = 256


def dot(left, right, left_dim=1, right_dim=0):
    return contract(left, right, left_dim, right_dim)


def project_kernel(q_blocks, k_blocks, _, low, high, weight, cosine, sine, gains, *refs):
    out, saved, normed = refs[3:]
    block = pl.program_id(0)

    @pl.when(block == 0)
    def _():
        normed[: low.shape[0]] = low[...]
        normed[low.shape[0] :] = high[...]

    projected = dot(normed[...], weight[...])

    @pl.when(block < q_blocks + k_blocks)
    def _():
        saved[...] = projected
        gain = jnp.where(block < q_blocks, gains[0:1], gains[1:2])
        for first in range(0, projected.shape[1], HD):
            normal = rms_norm(projected[:, first : first + HD])[0] * gain
            turned = pltpu.roll(normal, HD // 2, 1) * sine[...]
            out[:, first : first + HD] = (normal * cosine[...] + turned).astype(bf16)

    @pl.when(block >= q_blocks + k_blocks)
    def _():
        out[...] = projected.astype(bf16)


def project(owner, halves, weight, cosine, sine, gains, into, q_cols, k_cols):
    depth, columns = weight.shape
    own_rows = 2 * halves[1].shape[0]
    step = min(k_cols, 256)
    q_blocks, k_blocks = q_cols // step, k_cols // step
    grid = columns // step
    whole = lambda j, o: (0, 0)
    return pl.pallas_call(
        lambda *refs: project_kernel(q_blocks, k_blocks, *refs),
        out_shape=tuple(jax.ShapeDtypeStruct(a.shape, a.dtype) for a in into),
        grid_spec=pltpu.PrefetchScalarGridSpec(
            num_scalar_prefetch=1,
            grid=(grid,),
            in_specs=[
                pl.BlockSpec((own_rows // 2, depth), whole),
                pl.BlockSpec((own_rows // 2, depth), whole),
                pl.BlockSpec((depth, step), lambda j, o: (0, j)),
                pl.BlockSpec((own_rows, HD), whole),
                pl.BlockSpec((own_rows, HD), whole),
                pl.BlockSpec((2, HD), whole),
                pl.BlockSpec(memory_space=pl.ANY),
                pl.BlockSpec(memory_space=pl.ANY),
                pl.BlockSpec(memory_space=pl.ANY),
            ],
            out_specs=(
                pl.BlockSpec((own_rows, step), lambda j, o: (o[0], j)),
                pl.BlockSpec(
                    (own_rows, step),
                    lambda j, o: (o[0], jnp.minimum(j, q_blocks + k_blocks - 1)),
                ),
                pl.BlockSpec((own_rows, depth), lambda j, o: (o[0], 0)),
            ),
        ),
        input_output_aliases={7: 0, 8: 1, 9: 2},
        compiler_params=pltpu.CompilerParams(vmem_limit_bytes=VMEM_LIMIT),
        cost_estimate=COST,
    )(owner, *halves, weight, cosine, sine, gains, *into)


def out_kernel(attended, x, weight, gain, hidden_rows, mlp_rows):
    step = pl.program_id(0)
    tile = weight.shape[1]
    here = pl.ds(pl.multiple_of(step * tile, tile), tile)
    hidden_rows[:, here] = x[:, here].astype(f32) + dot(attended[...], weight[...])

    @pl.when(step == pl.num_programs(0) - 1)
    def _():
        mlp_rows[...] = (rms_norm(hidden_rows[...])[0] * gain[...]).astype(bf16)


def out_project(attended, weight, x, gain):
    rows, width = x.shape
    tile = min(512, width)
    full = pl.BlockSpec((rows, width), lambda j: (0, 0))
    return pl.pallas_call(
        out_kernel,
        out_shape=(
            jax.ShapeDtypeStruct((rows, width), f32),
            jax.ShapeDtypeStruct((rows, width), bf16),
        ),
        grid=(width // tile,),
        in_specs=[
            pl.BlockSpec(attended.shape, lambda j: (0, 0)),
            full,
            pl.BlockSpec((weight.shape[0], tile), lambda j: (0, j)),
            pl.BlockSpec((1, width), lambda j: (0, 0)),
        ],
        out_specs=(full, full),
        compiler_params=pltpu.CompilerParams(vmem_limit_bytes=VMEM_LIMIT),
        cost_estimate=COST,
    )(attended, x, weight, gain[None])


def out_back_kernel(count, part, passed, cotangent, hidden_rows, gain, weight, *outs):
    rows_grad, branch, gain_grad, pieces = outs[0], outs[1], outs[2], outs[3:]
    step = pl.program_id(0)

    @pl.when(step == 0)
    def _():
        grad = part[...] + passed[...].astype(f32)
        normal, scale = rms_norm(hidden_rows[...])
        total = cotangent[...].astype(f32) + rms_back(grad, gain[...], normal, scale)
        rows_grad[...] = total
        branch[...] = total.astype(bf16)
        gain_grad[...] = jnp.sum(grad * normal, axis=0, keepdims=True)

    piece = dot(branch[...], weight[...], 1, 1).astype(bf16)
    for k in range(count):

        @pl.when(step == k)
        def _(k=k):
            pieces[k][...] = piece


def out_back(count, part, passed, cotangent, hidden_rows, gain, weight):
    rows, width = part.shape
    cols = weight.shape[0] // count
    full = pl.BlockSpec((rows, width), lambda j: (0, 0))
    line = pl.BlockSpec((1, width), lambda j: (0, 0))
    results = pl.pallas_call(
        lambda *refs: out_back_kernel(count, *refs),
        out_shape=(
            jax.ShapeDtypeStruct((rows, width), f32),
            jax.ShapeDtypeStruct((rows, width), bf16),
            jax.ShapeDtypeStruct((1, width), f32),
        )
        + (jax.ShapeDtypeStruct((rows, cols), bf16),) * count,
        grid=(count,),
        in_specs=[full, full, full, full, line, pl.BlockSpec((cols, width), lambda j: (j, 0))],
        out_specs=(full, full, line) + (pl.BlockSpec((rows, cols), lambda j: (0, 0)),) * count,
        compiler_params=pltpu.CompilerParams(vmem_limit_bytes=VMEM_LIMIT),
        cost_estimate=COST,
    )(part, passed, cotangent, hidden_rows, gain[None], weight)
    return results[0], results[1], results[2][0], list(results[3:])


def feed_kernel(rows_in, low, high, w_gate, w_up, w_down, *refs):
    hidden, grads, all_in, all_cot, part = refs[4:]
    step = pl.program_id(0)

    @pl.when(step == 0)
    def _():
        all_in[...] = rows_in[...]
        all_cot[: low.shape[0]] = low[...]
        all_cot[low.shape[0] :] = high[...]

    tile = w_gate.shape[1]
    units = grads.shape[1] // 2
    gate_act = dot(rows_in[...], w_gate[...])
    up_act = dot(rows_in[...], w_up[...])
    hidden_grad = dot(all_cot[...], w_down[...])
    sigmoid = jax.nn.sigmoid(gate_act)
    silu = gate_act * sigmoid
    hidden[...] = (silu * up_act).astype(bf16)
    gate_grad = hidden_grad * up_act * sigmoid * (1.0 + gate_act * (1.0 - sigmoid))
    gate_grad = gate_grad.astype(bf16)
    up_grad = (hidden_grad * silu).astype(bf16)
    first = pl.multiple_of(step * tile, tile)
    grads[:, pl.ds(first, tile)] = gate_grad
    grads[:, pl.ds(pl.multiple_of(units + first, tile), tile)] = up_grad
    more = dot(gate_grad, w_gate[...], 1, 1) + dot(up_grad, w_up[...], 1, 1)

    @pl.when(step == 0)
    def _():
        part[...] = more

    @pl.when(step > 0)
    def _():
        part[...] += more


def feed(index, rows_in, halves, weights, into):
    rows, width = rows_in.shape
    units = into[0].shape[1]
    tile = 512 if units % 512 == 0 else 256
    steps = units // tile
    full = pl.BlockSpec((rows, width), lambda j: (0, 0))
    here = pl.BlockSpec((rows, width), lambda j: (index, 0))
    *into, part = pl.pallas_call(
        feed_kernel,
        out_shape=tuple(jax.ShapeDtypeStruct(a.shape, a.dtype) for a in into)
        + (jax.ShapeDtypeStruct((rows, width), f32),),
        grid=(steps,),
        in_specs=[
            full,
            pl.BlockSpec((rows // 2, width), lambda j: (0, 0)),
            pl.BlockSpec((rows // 2, width), lambda j: (0, 0)),
            pl.BlockSpec((width, tile), lambda j: (0, j)),
            pl.BlockSpec((width, tile), lambda j: (0, steps + j)),
            pl.BlockSpec((width, tile), lambda j: (0, 2 * steps + j)),
        ]
        + [pl.BlockSpec(memory_space=pl.ANY)] * 4,
        out_specs=(
            pl.BlockSpec((rows, tile), lambda j: (index, j)),
            pl.BlockSpec((rows, 2 * units), lambda j: (index, 0)),
            here,
            here,
            full,
        ),
        input_output_aliases={6: 0, 7: 1, 8: 2, 9: 3},
        compiler_params=pltpu.CompilerParams(vmem_limit_bytes=VMEM_LIMIT),
        cost_estimate=COST,
    )(rows_in, *halves, weights, weights, weights, *into)
    return tuple(into), part


def weight_grad_kernel(left, right, out):
    out[...] = dot(left[...], right[...], 0, 0).astype(bf16)


def weight_grad(left, right):
    rows, height = left.shape
    width = right.shape[1]
    tile = 512 if width % 512 == 0 else 256
    return pl.pallas_call(
        weight_grad_kernel,
        out_shape=jax.ShapeDtypeStruct((height, width), bf16),
        grid=(width // tile,),
        in_specs=[
            pl.BlockSpec((rows, height), lambda j: (0, 0)),
            pl.BlockSpec((rows, tile), lambda j: (0, j)),
        ],
        out_specs=pl.BlockSpec((height, tile), lambda j: (0, j)),
        compiler_params=pltpu.CompilerParams(vmem_limit_bytes=VMEM_LIMIT),
        cost_estimate=COST,
    )(left, right)


def head_weight_grad_kernel(normed, q_grad, k_grad, v_grad, weight, out, gain):
    first, gain_total = 0, 0.0
    for grad in (q_grad, k_grad, v_grad):
        last = first + grad.shape[1]
        part = dot(normed[...], grad[...], 0, 0)
        out[:, first:last] = part.astype(bf16)
        product = part * weight[:, first:last].astype(f32)
        for column in range(0, last - first, HD):
            gain_total += product[:, column : column + HD]
        first = last
    gain[...] = gain_total


def head_weight_grad(normed, grads, weight):
    rows, width = normed.shape
    columns = weight.shape[1]
    tile = min(512, width)
    return pl.pallas_call(
        head_weight_grad_kernel,
        out_shape=(
            jax.ShapeDtypeStruct((width, columns), bf16),
            jax.ShapeDtypeStruct((width, HD), f32),
        ),
        grid=(width // tile,),
        in_specs=[pl.BlockSpec((rows, tile), lambda j: (0, j))]
        + [pl.BlockSpec(g.shape, lambda j: (0, 0)) for g in grads]
        + [pl.BlockSpec((tile, columns), lambda j: (j, 0))],
        out_specs=(
            pl.BlockSpec((tile, columns), lambda j: (j, 0)),
            pl.BlockSpec((tile, HD), lambda j: (j, 0)),
        ),
        compiler_params=pltpu.CompilerParams(vmem_limit_bytes=VMEM_LIMIT),
        cost_estimate=COST,
    )(normed, *grads, weight)


def down_kernel(hidden, weight, *refs):
    total = dot(hidden[...], weight[...], 1, 1)
    for more in refs[:-1]:
        total += more[...].astype(f32)
    refs[-1][...] = total.astype(refs[-1].dtype)


def down_project(index, hidden, weights, *more, dtype=bf16):
    width, units = weights.shape[0], hidden.shape[1]
    rows = more[0].shape[0] if more else hidden.shape[0] // lax.axis_size("tensor")
    tile = min(512, width)
    block = pl.BlockSpec((rows, tile), lambda j: (0, j))
    return pl.pallas_call(
        down_kernel,
        out_shape=jax.ShapeDtypeStruct((rows, width), dtype),
        grid=(width // tile,),
        in_specs=[
            pl.BlockSpec((rows, units), lambda j: (index, 0)),
            pl.BlockSpec((tile, units), lambda j: (j, 2)),
        ]
        + [block] * len(more),
        out_specs=block,
        compiler_params=pltpu.CompilerParams(vmem_limit_bytes=VMEM_LIMIT),
        cost_estimate=COST,
    )(hidden, weights, *more)


def masked_scores(query, key, first):
    scores = dot(query, key, 1, 1) * (HD ** (-0.5))
    row = lax.broadcasted_iota(jnp.int32, scores.shape, 0) + first
    return jnp.where(row >= lax.broadcasted_iota(jnp.int32, scores.shape, 1), scores, NEGATIVE)


def softmax(scores):
    exponent = jnp.exp(scores - jnp.max(scores, axis=1, keepdims=True))
    return exponent * (1.0 / jnp.sum(exponent, axis=1, keepdims=True))


def attend_kernel(queries, keys, values, out):
    rows = min(QUERY_ROWS, queries.shape[0])
    for first in range(0, queries.shape[0], rows):
        last = first + rows
        for head in range(0, queries.shape[1], HD):
            probs = softmax(
                masked_scores(queries[first:last, head : head + HD], keys[:last], first)
            )
            out[first:last, head : head + HD] = dot(probs.astype(bf16), values[:last]).astype(bf16)


def attend(qkv, length, q_cols, k_cols):
    rows = qkv.shape[0]
    groups = k_cols // HD
    share = q_cols // groups
    return pl.pallas_call(
        attend_kernel,
        out_shape=jax.ShapeDtypeStruct((rows, q_cols), bf16),
        grid=(rows // length, groups),
        in_specs=[
            pl.BlockSpec((length, share), lambda s, g: (s, g)),
            pl.BlockSpec((length, HD), lambda s, g: (s, q_cols // HD + g)),
            pl.BlockSpec((length, HD), lambda s, g: (s, (q_cols + k_cols) // HD + g)),
        ],
        out_specs=pl.BlockSpec((length, share), lambda s, g: (s, g)),
        compiler_params=pltpu.CompilerParams(vmem_limit_bytes=VMEM_LIMIT),
        cost_estimate=COST,
    )(qkv, qkv, qkv)


def unrope_unnorm(grad, projected, gain, cosine, sine):
    grad = grad * cosine + pltpu.roll(grad * sine, HD // 2, 1)
    normal, scale = rms_norm(projected)
    return rms_back(grad, gain, normal, scale), grad * normal


def attend_back_kernel(
    queries, keys, values, grads, q_proj, k_proj, cosine, sine, gains,
    q_out, k_out, v_out, gain_out, key_grad, value_grad,
):
    length = queries.shape[0]
    rows = min(QUERY_ROWS, length)
    scale = HD ** (-0.5)
    gain_total = jnp.zeros((1, HD), f32)
    for first in range(length - rows, -1, -rows):
        last = first + rows
        for head in range(0, queries.shape[1], HD):
            columns = slice(head, head + HD)
            query, grad = queries[first:last, columns], grads[first:last, columns]
            probs = softmax(masked_scores(query, keys[:last], first))
            prob_grad = dot(grad, values[:last], 1, 1)
            delta = jnp.sum(probs * prob_grad, axis=1, keepdims=True)
            score_grad = (probs * (prob_grad - delta)).astype(bf16)
            value_part = dot(probs.astype(bf16), grad, 0, 0)
            key_part = dot(score_grad, query, 0, 0)
            if last == length and head == 0:
                key_grad[...] = key_part
                value_grad[...] = value_part
            else:
                key_grad[:last] += key_part
                value_grad[:last] += value_part
            out, gain_rows = unrope_unnorm(
                dot(score_grad, keys[:last]) * scale,
                q_proj[first:last, columns],
                gains[0:1],
                cosine[first:last],
                sine[first:last],
            )
            q_out[first:last, columns] = out.astype(bf16)
            gain_total += jnp.sum(gain_rows, axis=0, keepdims=True)
    out, gain_rows = unrope_unnorm(
        key_grad[...] * scale, k_proj[...], gains[1:2], cosine[...], sine[...]
    )
    k_out[...] = out.astype(bf16)
    v_out[...] = value_grad[...].astype(bf16)
    gain_out[0, 0:1] = gain_total
    gain_out[0, 1:2] = jnp.sum(gain_rows, axis=0, keepdims=True)


def attend_back(qkv, grads, saved, cosine, sine, gains, length, q_cols, k_cols):
    rows = qkv.shape[0]
    groups = k_cols // HD
    share = q_cols // groups
    return pl.pallas_call(
        attend_back_kernel,
        out_shape=(
            jax.ShapeDtypeStruct((rows, q_cols), bf16),
            jax.ShapeDtypeStruct((rows, k_cols), bf16),
            jax.ShapeDtypeStruct((rows, k_cols), bf16),
            jax.ShapeDtypeStruct((rows // length * groups, 2, HD), f32),
        ),
        grid=(rows // length, groups),
        in_specs=[
            pl.BlockSpec((length, share), lambda s, g: (s, g)),
            pl.BlockSpec((length, HD), lambda s, g: (s, q_cols // HD + g)),
            pl.BlockSpec((length, HD), lambda s, g: (s, (q_cols + k_cols) // HD + g)),
            pl.BlockSpec((length, share), lambda s, g: (s, g)),
            pl.BlockSpec((length, share), lambda s, g: (s, g)),
            pl.BlockSpec((length, HD), lambda s, g: (s, q_cols // HD + g)),
            pl.BlockSpec((length, HD), lambda s, g: (s, 0)),
            pl.BlockSpec((length, HD), lambda s, g: (s, 0)),
            pl.BlockSpec((2, HD), lambda s, g: (0, 0)),
        ],
        out_specs=(
            pl.BlockSpec((length, share), lambda s, g: (s, g)),
            pl.BlockSpec((length, HD), lambda s, g: (s, g)),
            pl.BlockSpec((length, HD), lambda s, g: (s, g)),
            pl.BlockSpec((1, 2, HD), lambda s, g: (s * groups + g, 0, 0)),
        ),
        scratch_shapes=[pltpu.VMEM((length, HD), f32), pltpu.VMEM((length, HD), f32)],
        compiler_params=pltpu.CompilerParams(vmem_limit_bytes=VMEM_LIMIT),
        cost_estimate=COST,
    )(qkv, qkv, qkv, grads, saved, saved, cosine, sine, gains)


def normed_back_kernel(_, q_grad, k_grad, v_grad, weight, out):
    first, total = 0, None
    for grad in (q_grad, k_grad, v_grad):
        last = first + grad.shape[1]
        part = dot(grad[...], weight[:, first:last], 1, 1)
        total = part if total is None else total + part
        first = last
    out[...] = total.astype(out.dtype)


def normed_back(owner, grads, weight, own_rows, dtype=f32):
    width, columns = weight.shape
    tile = min(512, width)
    return pl.pallas_call(
        normed_back_kernel,
        out_shape=jax.ShapeDtypeStruct((own_rows, width), dtype),
        grid_spec=pltpu.PrefetchScalarGridSpec(
            num_scalar_prefetch=1,
            grid=(width // tile,),
            in_specs=[pl.BlockSpec((own_rows, g.shape[1]), lambda j, o: (o[0], 0)) for g in grads]
            + [pl.BlockSpec((tile, columns), lambda j, o: (j, 0))],
            out_specs=pl.BlockSpec((own_rows, tile), lambda j, o: (0, j)),
        ),
        compiler_params=pltpu.CompilerParams(vmem_limit_bytes=VMEM_LIMIT),
        cost_estimate=COST,
    )(owner, *grads, weight)


def per_device(
    tokens,
    positions,
    attn_gain,
    query_weight,
    key_weight,
    value_weight,
    query_gain,
    key_gain,
    out_weight,
    mlp_gain,
    gate_weight,
    up_weight,
    down_weight,
    cotangent,
):
    own_rows, width = tokens.shape
    count = lax.axis_size("tensor")
    place = lax.axis_index("tensor")
    length = LEN
    q_cols, k_cols = query_weight.shape[1], key_weight.shape[1]
    head_cols = out_weight.shape[0]
    units = gate_weight.shape[1]
    owners = lax.rem(place - jnp.arange(count, dtype=jnp.int32) + count, count)

    x_rows = tokens.astype(f32)
    x_normal, x_scale = rms_norm(x_rows)
    digits = jnp.stack([positions // 128, positions % 128]).astype(bf16)
    digits = jnp.pad(digits, ((0, 14), (0, width - own_rows)))
    normed_rows = (x_normal * attn_gain).astype(bf16)
    middle = own_rows // 2
    lows = [jnp.concatenate([normed_rows[:middle], digits], axis=0)]
    highs = [normed_rows[middle:]]

    w_qkv = lax.all_gather(
        jnp.concatenate([query_weight, key_weight, value_weight], axis=1), "dp", axis=0, tiled=True
    )
    out_rows = [out_weight]
    for step in range(1, count):
        pairs = [(i, (i + step) % count) for i in range(count)]
        out_rows.append(lax.ppermute(out_weight, "tensor", pairs))
    lows.append(pass_on(lows[-1], "tensor"))
    highs.append(pass_on(highs[-1], "tensor"))
    lows, highs, out_rows = fence(lows, highs, out_rows)
    w_out = lax.all_gather(jnp.concatenate(out_rows, axis=0), "dp", axis=1, tiled=True)

    group_rows = count * own_rows
    into = (
        jnp.zeros((group_rows, q_cols + 2 * k_cols), bf16),
        jnp.zeros((group_rows, q_cols + k_cols), f32),
        jnp.zeros((group_rows, width), bf16),
    )
    head_gains = jnp.stack([query_gain, key_gain])
    tables = []

    def project_block(step, into):
        digit_rows = lows[step][middle : middle + 2, :own_rows].astype(f32)
        tables.append(angle_tables(digit_rows[0] * 128.0 + digit_rows[1], HD))
        return project(
            owners[step : step + 1],
            (lows[step], highs[step]),
            w_qkv,
            *tables[-1],
            head_gains,
            into,
            q_cols,
            k_cols,
        )

    for step in range(2, count):
        lows.append(pass_on(lows[-1], "tensor"))
        highs.append(pass_on(highs[-1], "tensor"))
        for block in range(0 if step == 2 else step - 1, step):
            into = project_block(block, into)
        lows[step], highs[step], into = fence(lows[step], highs[step], into)
        if step == 2:
            w_feed = after((gate_weight, up_weight, down_weight), lows[step], highs[step])
            w_feed = lax.all_gather(
                jnp.concatenate([w_feed[0], w_feed[1], w_feed[2].T], axis=1),
                "dp",
                axis=0,
                tiled=True,
            )
    cot_low, cot_high = after((cotangent[:middle], cotangent[middle:]), lows[-1], highs[-1])
    cot_lows, cot_highs = [cot_low], [cot_high]
    cot_lows.append(pass_on(cot_low, "tensor"))
    into = project_block(count - 1, into)
    qkv, saved, normed = into
    cosine = in_order([pair[0] for pair in tables], "tensor", -1)
    sine = in_order([pair[1] for pair in tables], "tensor", -1)
    attended_heads = attend(qkv, length, q_cols, k_cols)
    attended_heads, cot_lows = fence(attended_heads, cot_lows)

    pieces = [rows_of(attended_heads, place, own_rows)]
    for step in range(1, count):
        piece = rows_of(attended_heads, lax.rem(place + step, count), own_rows)
        pieces.append(lax.ppermute(piece, "tensor", [(i, (i + step) % count) for i in range(count)]))
    pieces, cot_lows, cot_highs = fence(pieces, cot_lows, cot_highs)
    attended = jnp.concatenate(pieces, axis=1)
    cot_highs.append(pass_on(cot_highs[-1], "tensor"))
    hidden_rows, mlp_rows = out_project(attended, w_out, tokens, mlp_gain)

    into = (
        jnp.zeros((group_rows, units), bf16),
        jnp.zeros((group_rows, 2 * units), bf16),
        jnp.zeros((group_rows, width), bf16),
        jnp.zeros((group_rows, width), bf16),
    )
    ins, parts = [mlp_rows], []
    grad_sum = mixed_sum = None
    for step in range(count + 1):
        if step + 1 < count:
            ins.append(pass_on(ins[-1], "tensor"))
        if step and len(cot_highs) < count:
            cot_highs.append(pass_on(cot_highs[-1], "tensor"))
        if len(cot_lows) < count:
            cot_lows.append(pass_on(cot_lows[-1], "tensor"))
        if step == 2:
            grad_sum = pass_on(parts[1].astype(bf16), "tensor")
        elif step > 2:
            send = (parts[step - 1] + grad_sum.astype(f32)).astype(bf16)
            grad_sum = pass_on(send, "tensor")
        if step == 3:
            mixed_sum = pass_on(mixed_part.astype(bf16), "tensor")
        elif step > 3:
            mixed_sum = pass_on((mixed_part + mixed_sum.astype(f32)).astype(bf16), "tensor")
        for block in {0: [], 1: [0, 1], count: []}.get(step, [step]):
            into, part = feed(
                block, ins[block], (cot_lows[block], cot_highs[block]), w_feed, into
            )
            parts.append(part)
        if step >= 2:
            mixed_part = down_project(step - 1, into[0], w_feed, dtype=f32)
        if step == count:
            down_wgrad = weight_grad(into[3], into[0])
            gate_up_wgrad = weight_grad(into[2], into[1])
            grad_sum, mixed_sum, mixed_part, into, down_wgrad, gate_up_wgrad = fence(
                grad_sum, mixed_sum, mixed_part, into, down_wgrad, gate_up_wgrad
            )
        else:
            ins, cot_lows, cot_highs, into, parts, grad_sum, mixed_sum = fence(
                ins, cot_lows, cot_highs, into, parts, grad_sum, mixed_sum
            )
            if step >= 2:
                mixed_part = after(mixed_part, into)
    hidden = into[0]
    down_sum = lax.psum_scatter(down_wgrad, "dp", scatter_dimension=0, tiled=True)
    gate_up_sum = lax.psum_scatter(gate_up_wgrad, "dp", scatter_dimension=0, tiled=True)

    rows_grad, branch_grad, mlp_gain_part, pieces = out_back(
        count, parts[0], grad_sum, cotangent, hidden_rows, mlp_gain, w_out
    )
    for step in range(1, count):
        pieces[step] = lax.ppermute(
            pieces[step], "tensor", [(i, (i - step) % count) for i in range(count)]
        )
    out_sum = HalvingSum(weight_grad(branch_grad, attended), "dp").prepare()
    pieces, mixed_sum, out_sum.sends = fence(pieces, mixed_sum, out_sum.sends)
    heads_grad = in_order(pieces, "tensor", 1)

    mixed_sum = pass_on((mixed_part + mixed_sum.astype(f32)).astype(bf16), "tensor")
    out_sum.launch(rows_grad.size)
    *head_grads, gain_parts = attend_back(
        qkv, heads_grad, saved, cosine, sine, head_gains, length, q_cols, k_cols
    )
    head_grads, gain_parts, mixed_sum, out_sum.state = fence(
        head_grads, gain_parts, mixed_sum, out_sum.state
    )
    first_part = normed_back(owners[1:2], head_grads, w_qkv, own_rows, bf16)
    normed_sum = pass_on(first_part, "tensor")

    out_sum.prepare()
    head_grads, out_sum.sends = fence(head_grads, out_sum.sends, first_part)[:2]
    out_sum.launch(rows_grad.size)
    part = normed_back(owners[2 % count :][:1], head_grads, w_qkv, own_rows)
    qkv_wgrad, attn_gain_part = head_weight_grad(normed, head_grads, w_qkv)
    qkv_sum = HalvingSum(qkv_wgrad, "dp").prepare()
    gains = jnp.concatenate(
        [
            jnp.sum(attn_gain_part, axis=1) / attn_gain,
            mlp_gain_part,
            jnp.sum(gain_parts, axis=0).reshape(-1),
        ]
    ).reshape(-1, HD)
    normed_sum, part, out_sum.state, qkv_sum.sends, gains, down_sum = fence(
        normed_sum, part, out_sum.state, qkv_sum.sends, gains, down_sum
    )
    out_block = None
    for step in range(2, count):
        send = (part + normed_sum.astype(f32)).astype(bf16)
        normed_sum = pass_on(send, "tensor")
        out_sum.state, qkv_sum.state, head_grads = fence(
            out_sum.state, qkv_sum.state, head_grads, send
        )[:3]
        if step == 2:
            qkv_sum.launch(rows_grad.size)
            gains = jnp.sum(lax.all_gather(gains, "dp", axis=0), axis=0)
        elif qkv_sum.steps < qkv_sum.bits:
            qkv_sum.prepare().launch(rows_grad.size)
        if out_sum.steps < out_sum.bits:
            out_sum.prepare().launch(rows_grad.size)
        elif out_block is None:
            out_block = out_sum.total(bf16)
        if step == 2:
            mixed = down_project(0, hidden, w_feed, mixed_sum, hidden_rows)
            down_sum = down_sum.astype(f32).T
        part = normed_back(owners[(step + 1) % count :][:1], head_grads, w_qkv, own_rows)
        normed_sum, part, out_sum.state, qkv_sum.state, gains, out_block = fence(
            normed_sum, part, out_sum.state, qkv_sum.state, gains, out_block
        )

    gain_lines = -(-gains.size // (16 * head_cols)) * 16
    gains = jnp.pad(gains.reshape(-1), (0, gain_lines * head_cols - gains.size))
    gains = gains.reshape(gain_lines, head_cols)
    gains_high = gains.astype(bf16)
    gains_low = (gains - gains_high.astype(f32)).astype(bf16)
    gains = jnp.concatenate([gains_high, gains_low], axis=0)
    total = 0.0
    for other in range(count):
        piece = out_block[:, other * head_cols : (other + 1) * head_cols]
        piece = jnp.concatenate([piece, gains], axis=0)
        if other:
            pairs = [(i, (i - other) % count) for i in range(count)]
            piece = lax.ppermute(piece, "tensor", pairs)
        total = total + piece.astype(f32)
    gains = total[-2 * gain_lines : -gain_lines] + total[-gain_lines:]
    gains = gains.reshape(-1)
    out_total = total[: -2 * gain_lines].T
    qkv_sum = qkv_sum.total(f32)
    normed_grad = part + normed_sum.astype(f32)
    token_grad = (rows_grad + rms_back(normed_grad, attn_gain, x_normal, x_scale)).astype(bf16)
    return (
        mixed,
        token_grad,
        gains[:width],
        qkv_sum[:, :q_cols].astype(f32),
        qkv_sum[:, q_cols : q_cols + k_cols].astype(f32),
        qkv_sum[:, q_cols + k_cols :].astype(f32),
        gains[2 * width : 2 * width + HD],
        gains[2 * width + HD : 2 * width + 2 * HD],
        out_total,
        gains[width : 2 * width],
        gate_up_sum[:, :units].astype(f32),
        gate_up_sum[:, units:].astype(f32),
        down_sum,
    )


def solution(mesh):
    in_specs = (
        P(("dp", "tensor"), None),
        P(("dp", "tensor")),
        P(),
        P("dp", "tensor"),
        P("dp", "tensor"),
        P("dp", "tensor"),
        P(),
        P(),
        P("tensor", "dp"),
        P(),
        P("dp", "tensor"),
        P("dp", "tensor"),
        P("tensor", "dp"),
        P(("dp", "tensor"), None),
    )
    out_specs = (
        P(("dp", "tensor"), None),
        P(("dp", "tensor"), None),
        P(),
        P("dp", "tensor"),
        P("dp", "tensor"),
        P("dp", "tensor"),
        P(),
        P(),
        P("tensor", "dp"),
        P(),
        P("dp", "tensor"),
        P("dp", "tensor"),
        P("tensor", "dp"),
    )
    return jax.shard_map(
        per_device, mesh=mesh, in_specs=in_specs, out_specs=out_specs, check_vma=False
    )
```

```python
import jax
import jax.numpy as jnp
from jax import lax
from jax.experimental import pallas as pl
from jax.experimental.pallas import tpu as pltpu
from jax.sharding import PartitionSpec as P

HD = 128
LEN = 1024

EPSILON = 1e-06
NEGATIVE = -1e30

f32 = jnp.float32
bf16 = jnp.bfloat16


def rms_norm(vector):
    scale = lax.rsqrt(jnp.mean(vector * vector, axis=-1, keepdims=True) + EPSILON)
    return vector * scale, scale


def rms_back(grad, gains, normal, scale):
    weighted = grad * gains
    return scale * (weighted - normal * jnp.mean(weighted * normal, axis=-1, keepdims=True))


def angle_tables(places, width):
    frequency = 1000000.0 ** (-jnp.arange(0, width, 2, dtype=f32) / width)
    angles = places.astype(f32)[:, None] * frequency[None, :]
    cosine, sine = jnp.cos(angles), jnp.sin(angles)
    return (
        jnp.concatenate([cosine, cosine], axis=-1),
        jnp.concatenate([-sine, sine], axis=-1),
    )


def contract(left, right, left_dim, right_dim):
    return lax.dot_general(
        left, right, (((left_dim,), (right_dim,)), ((), ())), preferred_element_type=f32
    )


def fence(*trees):
    leaves, shape = jax.tree.flatten(trees)
    return jax.tree.unflatten(shape, lax.optimization_barrier(leaves))


def after(value, *others):
    return fence(value, others)[0]


def pass_on(value, axis):
    count = lax.axis_size(axis)
    return lax.ppermute(value, axis, [(i, (i + 1) % count) for i in range(count)])


def sum_kernel(count, columns, _, *refs):
    total = refs[0][:, :, :columns].astype(f32)
    for more in refs[1:count]:
        total += more[:, :, :columns].astype(f32)
    out = refs[-1]
    out[:, :, :columns] = total.astype(out.dtype)
    if len(refs) > count + 1:
        total = refs[count][...].astype(f32)
        for more in refs[1:count]:
            total += more[:, :, columns:].astype(f32)
        out[:, :, columns:] = total.astype(out.dtype)


def sum_blocks(places, arrays, half, rows, dtype, beside=None):
    size, columns = len(places[0]), arrays[0].shape[2]
    flat = jnp.stack([jnp.asarray(p, jnp.int32) for line in places for p in line])
    total = columns + (beside.shape[2] if beside is not None else 0)

    def spec(i):
        whole = arrays[i].shape[1] == rows
        return pl.BlockSpec(
            (1, rows, arrays[i].shape[2]),
            lambda k, at: (at[i * size + k], 0 if whole else half, 0),
        )

    specs = [spec(i) for i in range(len(arrays))]
    if beside is not None:
        whole = beside.shape[1] == rows
        specs.append(
            pl.BlockSpec(
                (1, rows, beside.shape[2]), lambda k, at: (0, 0 if whole else half, 0)
            )
        )
        arrays = list(arrays) + [beside]
    return pl.pallas_call(
        lambda *refs: sum_kernel(len(places), columns, *refs),
        out_shape=jax.ShapeDtypeStruct((size, rows, total), dtype),
        grid_spec=pltpu.PrefetchScalarGridSpec(
            num_scalar_prefetch=1,
            grid=(size,),
            in_specs=specs,
            out_specs=pl.BlockSpec((1, rows, total), lambda k, at: (k, 0, 0)),
        ),
        compiler_params=pltpu.CompilerParams(vmem_limit_bytes=VMEM_LIMIT),
        cost_estimate=COST,
    )(flat, *arrays)


class HalvingSum:
    def __init__(self, blocks, axis, beside=None):
        self.axis, self.count = axis, lax.axis_size(axis)
        self.bits = self.count.bit_length() - 1
        assert self.count == 1 << self.bits
        self.rows = blocks.shape[0] // self.count
        self.beside = None if beside is None else beside[None]
        others = list(range(1, self.bits))
        self.orders = ([0] + others, [0] + others[::-1])
        self.state = (blocks.reshape((self.count, self.rows) + blocks.shape[1:]), [])
        self.steps = 0

    def mine(self, bit):
        return lax.rem(lax.div(lax.axis_index(self.axis), 1 << bit), 2)

    def addends(self, half, step, sent):
        order = self.orders[half]
        free = sorted(order[step + 1 :]) if sent else []
        blocks = []
        for number in range(1 << len(free)):
            value = {bit: (number >> rank) & 1 for rank, bit in enumerate(free)}
            for bit in order:
                if bit not in value:
                    value[bit] = self.mine(bit)
            if sent:
                value[order[step]] = 1 - value[order[step]]
            blocks.append(value)
        arrays = [(self.state[0], sorted(order))]
        for before, arrived in enumerate(self.state[1]):
            pieces = arrived[min(half, len(arrived) - 1)]
            pieces = pieces[0] if len(pieces) == 1 else jnp.concatenate(pieces, axis=0)
            arrays.append((pieces, sorted(order[before + 1 :])))
        places = [
            [sum((v[bit] << rank for rank, bit in enumerate(bits)), jnp.int32(0)) for v in blocks]
            for _, bits in arrays
        ]
        return places, [array for array, _ in arrays]

    def prepare(self):
        first = self.steps == 0
        self.sends = []
        for half in range(1 if first else 2):
            places, arrays = self.addends(half, self.steps, True)
            rows = self.rows if first else self.rows // 2
            self.sends.append(sum_blocks(places, arrays, half, rows, bf16, self.beside))
        return self

    def launch(self, piece_size):
        arrived = []
        for half, send in enumerate(self.sends):
            bit = self.orders[half][self.steps]
            pairs = [(i, i ^ (1 << bit)) for i in range(self.count)]
            parts = max(1, send.size // piece_size)
            pieces = jnp.split(send, parts) if send.shape[0] % parts == 0 else [send]
            arrived.append([lax.ppermute(piece, self.axis, pairs) for piece in pieces])
        self.state = (self.state[0], self.state[1] + [arrived])
        self.steps += 1
        return self

    def step(self):
        return self if self.steps == self.bits else self.prepare().launch(self.state[0].size)

    def total(self, dtype):
        while self.steps < self.bits:
            self.step()
        halves = []
        for half in range(2):
            places, arrays = self.addends(half, self.bits, False)
            halves.append(sum_blocks(places, arrays, half, self.rows // 2, dtype, self.beside)[0])
        return jnp.concatenate(halves, axis=0)


def butterfly_sum(value, axis):
    count = lax.axis_size(axis)
    assert count & (count - 1) == 0
    bit = 1
    while bit < count:
        value = value + lax.ppermute(value, axis, [(i, i ^ bit) for i in range(count)])
        bit *= 2
    return value


def rows_of(array, index, rows):
    return lax.dynamic_slice_in_dim(array, index * rows, rows, axis=0)


def in_order(blocks, axis, sign, dim=0):
    count = lax.axis_size(axis)
    place = lax.axis_index(axis)
    size = blocks[0].shape[dim]
    shape = list(blocks[0].shape)
    shape[dim] *= count
    whole = jnp.zeros(shape, blocks[0].dtype)
    for step, block in enumerate(blocks):
        owner = lax.rem(place + sign * step + count, count)
        whole = lax.dynamic_update_slice_in_dim(whole, block, owner * size, axis=dim)
    return whole


VMEM_LIMIT = 48 * 2**20
COST = pl.CostEstimate(flops=2**20, bytes_accessed=2**20, transcendentals=0)
QUERY_ROWS = 256


def dot(left, right, left_dim=1, right_dim=0):
    return contract(left, right, left_dim, right_dim)


def project_kernel(q_blocks, k_blocks, _, low, high, weight, cosine, sine, gains, *refs):
    out, saved, normed = refs[3:]
    block = pl.program_id(0)

    @pl.when(block == 0)
    def _():
        normed[: low.shape[0]] = low[...]
        normed[low.shape[0] :] = high[...]

    projected = dot(normed[...], weight[...])

    @pl.when(block < q_blocks + k_blocks)
    def _():
        saved[...] = projected
        gain = jnp.where(block < q_blocks, gains[0:1], gains[1:2])
        for first in range(0, projected.shape[1], HD):
            normal = rms_norm(projected[:, first : first + HD])[0] * gain
            turned = pltpu.roll(normal, HD // 2, 1) * sine[...]
            out[:, first : first + HD] = (normal * cosine[...] + turned).astype(bf16)

    @pl.when(block >= q_blocks + k_blocks)
    def _():
        out[...] = projected.astype(bf16)


def project(owner, halves, weight, cosine, sine, gains, into, q_cols, k_cols):
    depth, columns = weight.shape
    own_rows = 2 * halves[1].shape[0]
    step = min(k_cols, 256)
    q_blocks, k_blocks = q_cols // step, k_cols // step
    grid = columns // step
    whole = lambda j, o: (0, 0)
    return pl.pallas_call(
        lambda *refs: project_kernel(q_blocks, k_blocks, *refs),
        out_shape=tuple(jax.ShapeDtypeStruct(a.shape, a.dtype) for a in into),
        grid_spec=pltpu.PrefetchScalarGridSpec(
            num_scalar_prefetch=1,
            grid=(grid,),
            in_specs=[
                pl.BlockSpec((own_rows // 2, depth), whole),
                pl.BlockSpec((own_rows // 2, depth), whole),
                pl.BlockSpec((depth, step), lambda j, o: (0, j)),
                pl.BlockSpec((own_rows, HD), whole),
                pl.BlockSpec((own_rows, HD), whole),
                pl.BlockSpec((2, HD), whole),
                pl.BlockSpec(memory_space=pl.ANY),
                pl.BlockSpec(memory_space=pl.ANY),
                pl.BlockSpec(memory_space=pl.ANY),
            ],
            out_specs=(
                pl.BlockSpec((own_rows, step), lambda j, o: (o[0], j)),
                pl.BlockSpec(
                    (own_rows, step),
                    lambda j, o: (o[0], jnp.minimum(j, q_blocks + k_blocks - 1)),
                ),
                pl.BlockSpec((own_rows, depth), lambda j, o: (o[0], 0)),
            ),
        ),
        input_output_aliases={7: 0, 8: 1, 9: 2},
        compiler_params=pltpu.CompilerParams(vmem_limit_bytes=VMEM_LIMIT),
        cost_estimate=COST,
    )(owner, *halves, weight, cosine, sine, gains, *into)


def out_kernel(attended, x, weight, gain, hidden_rows, mlp_rows):
    step = pl.program_id(0)
    tile = weight.shape[1]
    here = pl.ds(pl.multiple_of(step * tile, tile), tile)
    hidden_rows[:, here] = x[:, here].astype(f32) + dot(attended[...], weight[...])

    @pl.when(step == pl.num_programs(0) - 1)
    def _():
        mlp_rows[...] = (rms_norm(hidden_rows[...])[0] * gain[...]).astype(bf16)


def out_project(attended, weight, x, gain):
    rows, width = x.shape
    tile = min(512, width)
    full = pl.BlockSpec((rows, width), lambda j: (0, 0))
    return pl.pallas_call(
        out_kernel,
        out_shape=(
            jax.ShapeDtypeStruct((rows, width), f32),
            jax.ShapeDtypeStruct((rows, width), bf16),
        ),
        grid=(width // tile,),
        in_specs=[
            pl.BlockSpec(attended.shape, lambda j: (0, 0)),
            full,
            pl.BlockSpec((weight.shape[0], tile), lambda j: (0, j)),
            pl.BlockSpec((1, width), lambda j: (0, 0)),
        ],
        out_specs=(full, full),
        compiler_params=pltpu.CompilerParams(vmem_limit_bytes=VMEM_LIMIT),
        cost_estimate=COST,
    )(attended, x, weight, gain[None])


def out_back_kernel(count, part, passed, cotangent, hidden_rows, gain, weight, *outs):
    rows_grad, branch, gain_grad, pieces = outs[0], outs[1], outs[2], outs[3:]
    step = pl.program_id(0)

    @pl.when(step == 0)
    def _():
        grad = part[...] + passed[...].astype(f32)
        normal, scale = rms_norm(hidden_rows[...])
        total = cotangent[...].astype(f32) + rms_back(grad, gain[...], normal, scale)
        rows_grad[...] = total
        branch[...] = total.astype(bf16)
        gain_grad[...] = jnp.sum(grad * normal, axis=0, keepdims=True)

    piece = dot(branch[...], weight[...], 1, 1).astype(bf16)
    for k in range(count):

        @pl.when(step == k)
        def _(k=k):
            pieces[k][...] = piece


def out_back(count, part, passed, cotangent, hidden_rows, gain, weight):
    rows, width = part.shape
    cols = weight.shape[0] // count
    full = pl.BlockSpec((rows, width), lambda j: (0, 0))
    line = pl.BlockSpec((1, width), lambda j: (0, 0))
    results = pl.pallas_call(
        lambda *refs: out_back_kernel(count, *refs),
        out_shape=(
            jax.ShapeDtypeStruct((rows, width), f32),
            jax.ShapeDtypeStruct((rows, width), bf16),
            jax.ShapeDtypeStruct((1, width), f32),
        )
        + (jax.ShapeDtypeStruct((rows, cols), bf16),) * count,
        grid=(count,),
        in_specs=[full, full, full, full, line, pl.BlockSpec((cols, width), lambda j: (j, 0))],
        out_specs=(full, full, line) + (pl.BlockSpec((rows, cols), lambda j: (0, 0)),) * count,
        compiler_params=pltpu.CompilerParams(vmem_limit_bytes=VMEM_LIMIT),
        cost_estimate=COST,
    )(part, passed, cotangent, hidden_rows, gain[None], weight)
    return results[0], results[1], results[2][0], list(results[3:])


def feed_kernel(rows_in, low, high, w_gate, w_up, w_down, *refs):
    hidden, grads, all_in, all_cot, part = refs[4:]
    step = pl.program_id(0)

    @pl.when(step == 0)
    def _():
        all_in[...] = rows_in[...]
        all_cot[: low.shape[0]] = low[...]
        all_cot[low.shape[0] :] = high[...]

    tile = w_gate.shape[1]
    units = grads.shape[1] // 2
    gate_act = dot(rows_in[...], w_gate[...])
    up_act = dot(rows_in[...], w_up[...])
    hidden_grad = dot(all_cot[...], w_down[...])
    sigmoid = jax.nn.sigmoid(gate_act)
    silu = gate_act * sigmoid
    hidden[...] = (silu * up_act).astype(bf16)
    gate_grad = hidden_grad * up_act * sigmoid * (1.0 + gate_act * (1.0 - sigmoid))
    gate_grad = gate_grad.astype(bf16)
    up_grad = (hidden_grad * silu).astype(bf16)
    first = pl.multiple_of(step * tile, tile)
    grads[:, pl.ds(first, tile)] = gate_grad
    grads[:, pl.ds(pl.multiple_of(units + first, tile), tile)] = up_grad
    more = dot(gate_grad, w_gate[...], 1, 1) + dot(up_grad, w_up[...], 1, 1)

    @pl.when(step == 0)
    def _():
        part[...] = more

    @pl.when(step > 0)
    def _():
        part[...] += more


def feed(index, rows_in, halves, weights, into):
    rows, width = rows_in.shape
    units = into[0].shape[1]
    tile = 512 if units % 512 == 0 else 256
    steps = units // tile
    full = pl.BlockSpec((rows, width), lambda j: (0, 0))
    here = pl.BlockSpec((rows, width), lambda j: (index, 0))
    *into, part = pl.pallas_call(
        feed_kernel,
        out_shape=tuple(jax.ShapeDtypeStruct(a.shape, a.dtype) for a in into)
        + (jax.ShapeDtypeStruct((rows, width), f32),),
        grid=(steps,),
        in_specs=[
            full,
            pl.BlockSpec(halves[0].shape, lambda j: (0, 0)),
            pl.BlockSpec(halves[1].shape, lambda j: (0, 0)),
            pl.BlockSpec((width, tile), lambda j: (0, j)),
            pl.BlockSpec((width, tile), lambda j: (0, steps + j)),
            pl.BlockSpec((width, tile), lambda j: (0, 2 * steps + j)),
        ]
        + [pl.BlockSpec(memory_space=pl.ANY)] * 4,
        out_specs=(
            pl.BlockSpec((rows, tile), lambda j: (index, j)),
            pl.BlockSpec((rows, 2 * units), lambda j: (index, 0)),
            here,
            here,
            full,
        ),
        input_output_aliases={6: 0, 7: 1, 8: 2, 9: 3},
        compiler_params=pltpu.CompilerParams(vmem_limit_bytes=VMEM_LIMIT),
        cost_estimate=COST,
    )(rows_in, *halves, weights, weights, weights, *into)
    return tuple(into), part


def weight_grad_kernel(left, right, *refs):
    refs[-1][...] = dot(left[...], right[...], 0, 0).astype(bf16)


def weight_grad(left, right, columns=None, first=0, into=None):
    rows, height = left.shape
    width = right.shape[1]
    tile = 512 if width % 512 == 0 else 256
    skip = first // tile
    return pl.pallas_call(
        weight_grad_kernel,
        out_shape=jax.ShapeDtypeStruct((height, columns or width), bf16),
        grid=(width // tile,),
        in_specs=[
            pl.BlockSpec((rows, height), lambda j: (0, 0)),
            pl.BlockSpec((rows, tile), lambda j: (0, j)),
        ]
        + [pl.BlockSpec(memory_space=pl.ANY)] * (into is not None),
        out_specs=pl.BlockSpec((height, tile), lambda j: (0, skip + j)),
        input_output_aliases={} if into is None else {2: 0},
        compiler_params=pltpu.CompilerParams(vmem_limit_bytes=VMEM_LIMIT),
        cost_estimate=COST,
    )(left, right, *([] if into is None else [into]))


def head_weight_grad_kernel(normed, q_grad, k_grad, v_grad, weight, out, gain):
    first, gain_total = 0, 0.0
    for grad in (q_grad, k_grad, v_grad):
        last = first + grad.shape[1]
        part = dot(normed[...], grad[...], 0, 0)
        out[:, first:last] = part.astype(bf16)
        product = part * weight[:, first:last].astype(f32)
        for column in range(0, last - first, HD):
            gain_total += product[:, column : column + HD]
        first = last
    gain[...] = gain_total


def head_weight_grad(normed, grads, weight):
    rows, width = normed.shape
    columns = weight.shape[1]
    tile = min(512, width)
    return pl.pallas_call(
        head_weight_grad_kernel,
        out_shape=(
            jax.ShapeDtypeStruct((width, columns), bf16),
            jax.ShapeDtypeStruct((width, HD), f32),
        ),
        grid=(width // tile,),
        in_specs=[pl.BlockSpec((rows, tile), lambda j: (0, j))]
        + [pl.BlockSpec(g.shape, lambda j: (0, 0)) for g in grads]
        + [pl.BlockSpec((tile, columns), lambda j: (j, 0))],
        out_specs=(
            pl.BlockSpec((tile, columns), lambda j: (j, 0)),
            pl.BlockSpec((tile, HD), lambda j: (j, 0)),
        ),
        compiler_params=pltpu.CompilerParams(vmem_limit_bytes=VMEM_LIMIT),
        cost_estimate=COST,
    )(normed, *grads, weight)


def down_kernel(hidden, weight, *refs):
    total = dot(hidden[...], weight[...], 1, 1)
    for more in refs[:-1]:
        total += more[...].astype(f32)
    refs[-1][...] = total.astype(refs[-1].dtype)


def down_project(index, hidden, weights, *more, dtype=bf16):
    width, units = weights.shape[0], hidden.shape[1]
    rows = more[0].shape[0] if more else hidden.shape[0] // lax.axis_size("tensor")
    tile = min(512, width)
    block = pl.BlockSpec((rows, tile), lambda j: (0, j))
    return pl.pallas_call(
        down_kernel,
        out_shape=jax.ShapeDtypeStruct((rows, width), dtype),
        grid=(width // tile,),
        in_specs=[
            pl.BlockSpec((rows, units), lambda j: (index, 0)),
            pl.BlockSpec((tile, units), lambda j: (j, 2)),
        ]
        + [block] * len(more),
        out_specs=block,
        compiler_params=pltpu.CompilerParams(vmem_limit_bytes=VMEM_LIMIT),
        cost_estimate=COST,
    )(hidden, weights, *more)


def masked_scores(query, key, first):
    scores = dot(query, key, 1, 1) * (HD ** (-0.5))
    row = lax.broadcasted_iota(jnp.int32, scores.shape, 0) + first
    return jnp.where(row >= lax.broadcasted_iota(jnp.int32, scores.shape, 1), scores, NEGATIVE)


def softmax(scores):
    exponent = jnp.exp(scores - jnp.max(scores, axis=1, keepdims=True))
    return exponent * (1.0 / jnp.sum(exponent, axis=1, keepdims=True))


def attend_kernel(queries, keys, values, out):
    rows = min(QUERY_ROWS, queries.shape[0])
    for first in range(0, queries.shape[0], rows):
        last = first + rows
        for head in range(0, queries.shape[1], HD):
            probs = softmax(
                masked_scores(queries[first:last, head : head + HD], keys[:last], first)
            )
            out[first:last, head : head + HD] = dot(probs.astype(bf16), values[:last]).astype(bf16)


def attend(qkv, length, q_cols, k_cols):
    rows = qkv.shape[0]
    groups = k_cols // HD
    share = q_cols // groups
    return pl.pallas_call(
        attend_kernel,
        out_shape=jax.ShapeDtypeStruct((rows, q_cols), bf16),
        grid=(rows // length, groups),
        in_specs=[
            pl.BlockSpec((length, share), lambda s, g: (s, g)),
            pl.BlockSpec((length, HD), lambda s, g: (s, q_cols // HD + g)),
            pl.BlockSpec((length, HD), lambda s, g: (s, (q_cols + k_cols) // HD + g)),
        ],
        out_specs=pl.BlockSpec((length, share), lambda s, g: (s, g)),
        compiler_params=pltpu.CompilerParams(vmem_limit_bytes=VMEM_LIMIT),
        cost_estimate=COST,
    )(qkv, qkv, qkv)


def unrope_unnorm(grad, projected, gain, cosine, sine):
    grad = grad * cosine + pltpu.roll(grad * sine, HD // 2, 1)
    normal, scale = rms_norm(projected)
    return rms_back(grad, gain, normal, scale), grad * normal


def attend_back_kernel(
    queries, keys, values, grads, q_proj, k_proj, cosine, sine, gains,
    q_out, k_out, v_out, gain_out, key_grad, value_grad,
):
    length = queries.shape[0]
    rows = min(QUERY_ROWS, length)
    scale = HD ** (-0.5)
    gain_total = jnp.zeros((1, HD), f32)
    for first in range(length - rows, -1, -rows):
        last = first + rows
        for head in range(0, queries.shape[1], HD):
            columns = slice(head, head + HD)
            query, grad = queries[first:last, columns], grads[first:last, columns]
            probs = softmax(masked_scores(query, keys[:last], first))
            prob_grad = dot(grad, values[:last], 1, 1)
            delta = jnp.sum(probs * prob_grad, axis=1, keepdims=True)
            score_grad = (probs * (prob_grad - delta)).astype(bf16)
            value_part = dot(probs.astype(bf16), grad, 0, 0)
            key_part = dot(score_grad, query, 0, 0)
            if last == length and head == 0:
                key_grad[...] = key_part
                value_grad[...] = value_part
            else:
                key_grad[:last] += key_part
                value_grad[:last] += value_part
            out, gain_rows = unrope_unnorm(
                dot(score_grad, keys[:last]) * scale,
                q_proj[first:last, columns],
                gains[0:1],
                cosine[first:last],
                sine[first:last],
            )
            q_out[first:last, columns] = out.astype(bf16)
            gain_total += jnp.sum(gain_rows, axis=0, keepdims=True)
    out, gain_rows = unrope_unnorm(
        key_grad[...] * scale, k_proj[...], gains[1:2], cosine[...], sine[...]
    )
    k_out[...] = out.astype(bf16)
    v_out[...] = value_grad[...].astype(bf16)
    gain_out[0, 0:1] = gain_total
    gain_out[0, 1:2] = jnp.sum(gain_rows, axis=0, keepdims=True)


def attend_back(qkv, grads, saved, cosine, sine, gains, length, q_cols, k_cols):
    rows = qkv.shape[0]
    groups = k_cols // HD
    share = q_cols // groups
    return pl.pallas_call(
        attend_back_kernel,
        out_shape=(
            jax.ShapeDtypeStruct((rows, q_cols), bf16),
            jax.ShapeDtypeStruct((rows, k_cols), bf16),
            jax.ShapeDtypeStruct((rows, k_cols), bf16),
            jax.ShapeDtypeStruct((rows // length * groups, 2, HD), f32),
        ),
        grid=(rows // length, groups),
        in_specs=[
            pl.BlockSpec((length, share), lambda s, g: (s, g)),
            pl.BlockSpec((length, HD), lambda s, g: (s, q_cols // HD + g)),
            pl.BlockSpec((length, HD), lambda s, g: (s, (q_cols + k_cols) // HD + g)),
            pl.BlockSpec((length, share), lambda s, g: (s, g)),
            pl.BlockSpec((length, share), lambda s, g: (s, g)),
            pl.BlockSpec((length, HD), lambda s, g: (s, q_cols // HD + g)),
            pl.BlockSpec((length, HD), lambda s, g: (s, 0)),
            pl.BlockSpec((length, HD), lambda s, g: (s, 0)),
            pl.BlockSpec((2, HD), lambda s, g: (0, 0)),
        ],
        out_specs=(
            pl.BlockSpec((length, share), lambda s, g: (s, g)),
            pl.BlockSpec((length, HD), lambda s, g: (s, g)),
            pl.BlockSpec((length, HD), lambda s, g: (s, g)),
            pl.BlockSpec((1, 2, HD), lambda s, g: (s * groups + g, 0, 0)),
        ),
        scratch_shapes=[pltpu.VMEM((length, HD), f32), pltpu.VMEM((length, HD), f32)],
        compiler_params=pltpu.CompilerParams(vmem_limit_bytes=VMEM_LIMIT),
        cost_estimate=COST,
    )(qkv, qkv, qkv, grads, saved, saved, cosine, sine, gains)


def normed_back_kernel(_, q_grad, k_grad, v_grad, weight, out):
    first, total = 0, None
    for grad in (q_grad, k_grad, v_grad):
        last = first + grad.shape[1]
        part = dot(grad[...], weight[:, first:last], 1, 1)
        total = part if total is None else total + part
        first = last
    out[...] = total.astype(out.dtype)


def normed_back(owner, grads, weight, own_rows, dtype=f32):
    width, columns = weight.shape
    tile = min(512, width)
    return pl.pallas_call(
        normed_back_kernel,
        out_shape=jax.ShapeDtypeStruct((own_rows, width), dtype),
        grid_spec=pltpu.PrefetchScalarGridSpec(
            num_scalar_prefetch=1,
            grid=(width // tile,),
            in_specs=[pl.BlockSpec((own_rows, g.shape[1]), lambda j, o: (o[0], 0)) for g in grads]
            + [pl.BlockSpec((tile, columns), lambda j, o: (j, 0))],
            out_specs=pl.BlockSpec((own_rows, tile), lambda j, o: (0, j)),
        ),
        compiler_params=pltpu.CompilerParams(vmem_limit_bytes=VMEM_LIMIT),
        cost_estimate=COST,
    )(owner, *grads, weight)


def per_device(
    tokens,
    positions,
    attn_gain,
    query_weight,
    key_weight,
    value_weight,
    query_gain,
    key_gain,
    out_weight,
    mlp_gain,
    gate_weight,
    up_weight,
    down_weight,
    cotangent,
):
    own_rows, width = tokens.shape
    count = lax.axis_size("tensor")
    place = lax.axis_index("tensor")
    length = LEN
    q_cols, k_cols = query_weight.shape[1], key_weight.shape[1]
    own_width = query_weight.shape[0]
    head_cols = out_weight.shape[0]
    units = gate_weight.shape[1]
    owners = lax.rem(place - jnp.arange(count, dtype=jnp.int32) + count, count)

    x_rows = tokens.astype(f32)
    x_normal, x_scale = rms_norm(x_rows)
    digits = jnp.stack([positions // 128, positions % 128]).astype(bf16)
    digits = jnp.pad(digits, ((0, 14), (0, width - own_rows)))
    normed_rows = (x_normal * attn_gain).astype(bf16)
    middle = own_rows // 2
    lows = [jnp.concatenate([normed_rows[:middle], digits], axis=0)]
    highs = [normed_rows[middle:]]

    heads_weight = after((query_weight, key_weight, value_weight), lows, highs)
    w_qkv = lax.all_gather(jnp.concatenate(heads_weight, axis=1), "dp", axis=0, tiled=True)
    out_rows = [out_weight]
    for step in range(1, count):
        pairs = [(i, (i + step) % count) for i in range(count)]
        out_rows.append(lax.ppermute(out_weight, "tensor", pairs))
    lows.append(pass_on(lows[-1], "tensor"))
    highs.append(pass_on(highs[-1], "tensor"))
    w_feed = after((gate_weight, up_weight, down_weight), out_rows[1])
    w_feed = jnp.concatenate([w_feed[0], w_feed[1], w_feed[2].T], axis=1)
    lows, highs, out_rows, w_feed = fence(lows, highs, out_rows, w_feed)
    w_out = jnp.concatenate(out_rows, axis=0)
    w_out, w_feed = fence(w_out, w_feed)
    w_out = lax.all_gather(w_out, "dp", axis=1, tiled=True)

    group_rows = count * own_rows
    into = (
        jnp.zeros((group_rows, q_cols + 2 * k_cols), bf16),
        jnp.zeros((group_rows, q_cols + k_cols), f32),
        jnp.zeros((group_rows, width), bf16),
    )
    head_gains = jnp.stack([query_gain, key_gain])
    tables = []

    def project_block(step, into):
        digit_rows = lows[step][middle : middle + 2, :own_rows].astype(f32)
        tables.append(angle_tables(digit_rows[0] * 128.0 + digit_rows[1], HD))
        return project(
            owners[step : step + 1],
            (lows[step], highs[step]),
            w_qkv,
            *tables[-1],
            head_gains,
            into,
            q_cols,
            k_cols,
        )

    for step in range(2, count):
        lows.append(pass_on(lows[-1], "tensor"))
        highs.append(pass_on(highs[-1], "tensor"))
        for block in range(0 if step == 2 else step - 1, step):
            into = project_block(block, into)
        lows[step], highs[step], into = fence(lows[step], highs[step], into)
        if step == 2:
            w_feed = lax.all_gather(after(w_feed, into), "dp", axis=0, tiled=True)
    split = own_rows * 3 // 4
    cot_low, cot_high = after((cotangent[:split], cotangent[split:]), lows[-1], highs[-1])
    cot_lows, cot_highs = [cot_low], [cot_high]
    cot_lows.append(pass_on(cot_low, "tensor"))
    into = project_block(count - 1, into)
    qkv, saved, normed = into
    cosine = in_order([pair[0] for pair in tables], "tensor", -1)
    sine = in_order([pair[1] for pair in tables], "tensor", -1)
    attended_heads = attend(qkv, length, q_cols, k_cols)
    attended_heads, cot_lows = fence(attended_heads, cot_lows)

    pieces = [rows_of(attended_heads, place, own_rows)]
    for step in range(1, count):
        piece = rows_of(attended_heads, lax.rem(place + step, count), own_rows)
        pieces.append(lax.ppermute(piece, "tensor", [(i, (i + step) % count) for i in range(count)]))
    pieces, cot_lows, cot_highs = fence(pieces, cot_lows, cot_highs)
    attended = jnp.concatenate(pieces, axis=1)
    cot_highs.append(pass_on(cot_highs[-1], "tensor"))
    hidden_rows, mlp_rows = out_project(attended, w_out, tokens, mlp_gain)

    into = (
        jnp.zeros((group_rows, units), bf16),
        jnp.zeros((group_rows, 2 * units), bf16),
        jnp.zeros((group_rows, width), bf16),
        jnp.zeros((group_rows, width), bf16),
    )
    ins, parts = [mlp_rows], []
    grad_sum = mixed_sum = None
    mixed_parts = []
    for step in range(count + 2):
        if step + 1 < count:
            ins.append(pass_on(ins[-1], "tensor"))
        if step and len(cot_highs) < count:
            cot_highs.append(pass_on(cot_highs[-1], "tensor"))
        if len(cot_lows) < count:
            cot_lows.append(pass_on(cot_lows[-1], "tensor"))
        if step > 2:
            send = parts[step - 2]
            if step > 3:
                send = send + grad_sum.astype(f32)
            grad_sum = pass_on(send.astype(bf16), "tensor")
        if 2 < step <= count:
            send = mixed_parts[step - 3]
            if step > 3:
                send = send + mixed_sum.astype(f32)
            mixed_sum = pass_on(send.astype(bf16), "tensor")
        for block in {0: [], 1: [0, 1], count: [], count + 1: []}.get(step, [step]):
            into, part = feed(
                block, ins[block], (cot_lows[block], cot_highs[block]), w_feed, into
            )
            parts.append(part)
        if step == 2:
            mixed_parts += [down_project(k, into[0], w_feed, dtype=f32) for k in range(1, 3)[: count - 1]]
        elif 3 < step <= count:
            mixed_parts.append(down_project(step - 1, into[0], w_feed, dtype=f32))
        if step == count - 1:
            feed_wgrad = weight_grad(into[2], into[1], 3 * units)
            feed_wgrad = weight_grad(into[3], into[0], 3 * units, 2 * units, feed_wgrad)
            into, feed_wgrad = fence(into, feed_wgrad)
        ins, cot_lows, cot_highs, into, parts, grad_sum, mixed_sum, mixed_parts = fence(
            ins, cot_lows, cot_highs, into, parts, grad_sum, mixed_sum, mixed_parts
        )
        if step == count - 1:
            feed_wgrad = after(feed_wgrad, into)
            feed_sum = lax.psum_scatter(feed_wgrad, "dp", scatter_dimension=0, tiled=True)
    hidden = into[0]

    rows_grad, branch_grad, mlp_gain_part, pieces = out_back(
        count, parts[0], grad_sum, cotangent, hidden_rows, mlp_gain, w_out
    )
    for step in range(1, count):
        pieces[step] = lax.ppermute(
            pieces[step], "tensor", [(i, (i - step) % count) for i in range(count)]
        )
    out_wgrad = weight_grad(branch_grad, attended)
    pieces, mixed_sum, out_wgrad = fence(pieces, mixed_sum, out_wgrad)
    heads_grad = in_order(pieces, "tensor", 1)
    out_block = lax.psum_scatter(out_wgrad, "dp", scatter_dimension=0, tiled=True)

    mixed_sum = pass_on((mixed_parts[-1] + mixed_sum.astype(f32)).astype(bf16), "tensor")
    *head_grads, gain_parts = attend_back(
        qkv, heads_grad, saved, cosine, sine, head_gains, length, q_cols, k_cols
    )
    head_grads, gain_parts, mixed_sum = fence(head_grads, gain_parts, mixed_sum)
    first_part = normed_back(owners[1:2], head_grads, w_qkv, own_rows, bf16)
    normed_sum = pass_on(first_part, "tensor")

    head_grads = after(head_grads, first_part)
    part = normed_back(owners[2 % count :][:1], head_grads, w_qkv, own_rows)
    qkv_wgrad, attn_gain_part = head_weight_grad(normed, head_grads, w_qkv)
    gains = jnp.concatenate(
        [
            jnp.sum(attn_gain_part, axis=1) / attn_gain,
            mlp_gain_part,
            jnp.sum(gain_parts, axis=0).reshape(-1),
        ]
    )
    beside_cols = -(-gains.size // (own_width // 2 * HD)) * HD
    beside = jnp.pad(gains, (0, own_width * beside_cols - gains.size))
    beside = beside.reshape(own_width, beside_cols).astype(bf16)
    qkv_sum = HalvingSum(qkv_wgrad, "dp", beside).prepare().launch(rows_grad.size // 2)
    normed_sum, part, qkv_sum.state, feed_sum = fence(
        normed_sum, part, qkv_sum.state, feed_sum
    )
    out_pieces = []
    for step in range(2, count):
        send = (part + normed_sum.astype(f32)).astype(bf16)
        normed_sum = pass_on(send, "tensor")
        qkv_sum.state, head_grads = fence(qkv_sum.state, head_grads, send)[:2]
        if qkv_sum.steps < qkv_sum.bits:
            qkv_sum.prepare().launch(rows_grad.size)
        if step == count - 1:
            out_block = after(out_block, send)
            out_pieces = [out_block[:, s * head_cols : (s + 1) * head_cols] for s in range(count)]
            mixed = down_project(0, hidden, w_feed, mixed_sum, hidden_rows)
            gate_sum = feed_sum[:, :units].astype(f32)
            up_sum = feed_sum[:, units : 2 * units].astype(f32)
            down_sum = feed_sum[:, 2 * units :].astype(f32).T
        part = normed_back(owners[(step + 1) % count :][:1], head_grads, w_qkv, own_rows)
        normed_sum, part, qkv_sum.state, out_pieces = fence(
            normed_sum, part, qkv_sum.state, out_pieces
        )

    for other in range(1, count):
        pairs = [(i, (i - other) % count) for i in range(count)]
        out_pieces[other] = lax.ppermute(out_pieces[other], "tensor", pairs)
    qkv_sum.state = after(qkv_sum.state, out_pieces[1])
    out_total = sum(piece.astype(f32) for piece in out_pieces).T
    qkv_sum = qkv_sum.total(f32)
    gains = qkv_sum[:, q_cols + 2 * k_cols :].reshape(-1)[: gains.size]
    gains = butterfly_sum(gains.reshape(-1, HD), "tensor").reshape(-1)
    normed_grad = part + normed_sum.astype(f32)
    token_grad = (rows_grad + rms_back(normed_grad, attn_gain, x_normal, x_scale)).astype(bf16)
    return (
        mixed,
        token_grad,
        gains[:width],
        qkv_sum[:, :q_cols],
        qkv_sum[:, q_cols : q_cols + k_cols],
        qkv_sum[:, q_cols + k_cols : q_cols + 2 * k_cols],
        gains[2 * width : 2 * width + HD],
        gains[2 * width + HD : 2 * width + 2 * HD],
        out_total,
        gains[width : 2 * width],
        gate_sum,
        up_sum,
        down_sum,
    )


def solution(mesh):
    in_specs = (
        P(("dp", "tensor"), None),
        P(("dp", "tensor")),
        P(),
        P("dp", "tensor"),
        P("dp", "tensor"),
        P("dp", "tensor"),
        P(),
        P(),
        P("tensor", "dp"),
        P(),
        P("dp", "tensor"),
        P("dp", "tensor"),
        P("tensor", "dp"),
        P(("dp", "tensor"), None),
    )
    out_specs = (
        P(("dp", "tensor"), None),
        P(("dp", "tensor"), None),
        P(),
        P("dp", "tensor"),
        P("dp", "tensor"),
        P("dp", "tensor"),
        P(),
        P(),
        P("tensor", "dp"),
        P(),
        P("dp", "tensor"),
        P("dp", "tensor"),
        P("tensor", "dp"),
    )
    return jax.shard_map(
        per_device, mesh=mesh, in_specs=in_specs, out_specs=out_specs, check_vma=False
    )
```

```python
import jax
import jax.numpy as jnp
from jax import lax
from jax.experimental import pallas as pl
from jax.experimental.pallas import tpu as pltpu
from jax.sharding import PartitionSpec as P

HD = 128
LEN = 1024

EPSILON = 1e-06
NEGATIVE = -1e30

f32 = jnp.float32
bf16 = jnp.bfloat16


def rms_norm(vector):
    scale = lax.rsqrt(jnp.mean(vector * vector, axis=-1, keepdims=True) + EPSILON)
    return vector * scale, scale


def rms_back(grad, gains, normal, scale):
    weighted = grad * gains
    return scale * (weighted - normal * jnp.mean(weighted * normal, axis=-1, keepdims=True))


def angle_tables(places, width):
    frequency = 1000000.0 ** (-jnp.arange(0, width, 2, dtype=f32) / width)
    angles = places.astype(f32)[:, None] * frequency[None, :]
    cosine, sine = jnp.cos(angles), jnp.sin(angles)
    return (
        jnp.concatenate([cosine, cosine], axis=-1),
        jnp.concatenate([-sine, sine], axis=-1),
    )


def contract(left, right, left_dim, right_dim):
    return lax.dot_general(
        left, right, (((left_dim,), (right_dim,)), ((), ())), preferred_element_type=f32
    )


def fence(*trees):
    leaves, shape = jax.tree.flatten(trees)
    return jax.tree.unflatten(shape, lax.optimization_barrier(leaves))


def after(value, *others):
    return fence(value, others)[0]


def pass_on(value, axis):
    count = lax.axis_size(axis)
    return lax.ppermute(value, axis, [(i, (i + 1) % count) for i in range(count)])


def sum_kernel(count, columns, _, *refs):
    total = refs[0][:, :, :columns].astype(f32)
    for more in refs[1:count]:
        total += more[:, :, :columns].astype(f32)
    out = refs[-1]
    out[:, :, :columns] = total.astype(out.dtype)
    if len(refs) > count + 1:
        total = refs[count][...].astype(f32)
        for more in refs[1:count]:
            total += more[:, :, columns:].astype(f32)
        out[:, :, columns:] = total.astype(out.dtype)


def sum_blocks(places, arrays, half, rows, dtype, beside=None):
    size, columns = len(places[0]), arrays[0].shape[2]
    flat = jnp.stack([jnp.asarray(p, jnp.int32) for line in places for p in line])
    total = columns + (beside.shape[2] if beside is not None else 0)

    def spec(i):
        whole = arrays[i].shape[1] == rows
        return pl.BlockSpec(
            (1, rows, arrays[i].shape[2]),
            lambda k, at: (at[i * size + k], 0 if whole else half, 0),
        )

    specs = [spec(i) for i in range(len(arrays))]
    if beside is not None:
        whole = beside.shape[1] == rows
        specs.append(
            pl.BlockSpec(
                (1, rows, beside.shape[2]), lambda k, at: (0, 0 if whole else half, 0)
            )
        )
        arrays = list(arrays) + [beside]
    return pl.pallas_call(
        lambda *refs: sum_kernel(len(places), columns, *refs),
        out_shape=jax.ShapeDtypeStruct((size, rows, total), dtype),
        grid_spec=pltpu.PrefetchScalarGridSpec(
            num_scalar_prefetch=1,
            grid=(size,),
            in_specs=specs,
            out_specs=pl.BlockSpec((1, rows, total), lambda k, at: (k, 0, 0)),
        ),
        compiler_params=pltpu.CompilerParams(vmem_limit_bytes=VMEM_LIMIT),
        cost_estimate=COST,
    )(flat, *arrays)


class HalvingSum:
    def __init__(self, blocks, axis, beside=None):
        self.axis, self.count = axis, lax.axis_size(axis)
        self.bits = self.count.bit_length() - 1
        assert self.count == 1 << self.bits
        self.rows = blocks.shape[0] // self.count
        self.beside = None if beside is None else beside[None]
        others = list(range(1, self.bits))
        self.orders = ([0] + others, [0] + others[::-1])
        self.state = (blocks.reshape((self.count, self.rows) + blocks.shape[1:]), [])
        self.steps = 0

    def mine(self, bit):
        return lax.rem(lax.div(lax.axis_index(self.axis), 1 << bit), 2)

    def addends(self, half, step, sent):
        order = self.orders[half]
        free = sorted(order[step + 1 :]) if sent else []
        blocks = []
        for number in range(1 << len(free)):
            value = {bit: (number >> rank) & 1 for rank, bit in enumerate(free)}
            for bit in order:
                if bit not in value:
                    value[bit] = self.mine(bit)
            if sent:
                value[order[step]] = 1 - value[order[step]]
            blocks.append(value)
        arrays = [(self.state[0], sorted(order))]
        for before, arrived in enumerate(self.state[1]):
            pieces = arrived[min(half, len(arrived) - 1)]
            pieces = pieces[0] if len(pieces) == 1 else jnp.concatenate(pieces, axis=0)
            arrays.append((pieces, sorted(order[before + 1 :])))
        places = [
            [sum((v[bit] << rank for rank, bit in enumerate(bits)), jnp.int32(0)) for v in blocks]
            for _, bits in arrays
        ]
        return places, [array for array, _ in arrays]

    def prepare(self):
        first = self.steps == 0
        self.sends = []
        for half in range(1 if first else 2):
            places, arrays = self.addends(half, self.steps, True)
            rows = self.rows if first else self.rows // 2
            self.sends.append(sum_blocks(places, arrays, half, rows, bf16, self.beside))
        return self

    def launch(self, piece_size):
        arrived = []
        for half, send in enumerate(self.sends):
            bit = self.orders[half][self.steps]
            pairs = [(i, i ^ (1 << bit)) for i in range(self.count)]
            parts = max(1, send.size // piece_size)
            pieces = jnp.split(send, parts) if send.shape[0] % parts == 0 else [send]
            arrived.append([lax.ppermute(piece, self.axis, pairs) for piece in pieces])
        self.state = (self.state[0], self.state[1] + [arrived])
        self.steps += 1
        return self

    def step(self):
        return self if self.steps == self.bits else self.prepare().launch(self.state[0].size)

    def total(self, dtype):
        while self.steps < self.bits:
            self.step()
        halves = []
        for half in range(2):
            places, arrays = self.addends(half, self.bits, False)
            halves.append(sum_blocks(places, arrays, half, self.rows // 2, dtype, self.beside)[0])
        return jnp.concatenate(halves, axis=0)


def butterfly_sum(value, axis):
    count = lax.axis_size(axis)
    assert count & (count - 1) == 0
    bit = 1
    while bit < count:
        value = value + lax.ppermute(value, axis, [(i, i ^ bit) for i in range(count)])
        bit *= 2
    return value


def rows_of(array, index, rows):
    return lax.dynamic_slice_in_dim(array, index * rows, rows, axis=0)


def in_order(blocks, axis, sign, dim=0):
    count = lax.axis_size(axis)
    place = lax.axis_index(axis)
    size = blocks[0].shape[dim]
    shape = list(blocks[0].shape)
    shape[dim] *= count
    whole = jnp.zeros(shape, blocks[0].dtype)
    for step, block in enumerate(blocks):
        owner = lax.rem(place + sign * step + count, count)
        whole = lax.dynamic_update_slice_in_dim(whole, block, owner * size, axis=dim)
    return whole


VMEM_LIMIT = 48 * 2**20
VMEM_WHOLE = 60 * 2**20
COST = pl.CostEstimate(flops=2**20, bytes_accessed=2**20, transcendentals=0)
QUERY_ROWS = 256


def dot(left, right, left_dim=1, right_dim=0):
    return contract(left, right, left_dim, right_dim)


def project_kernel(q_blocks, k_blocks, _, low, high, weight, cosine, sine, gains, *refs):
    out, saved, normed = refs[-3:]
    block = pl.program_id(0)

    @pl.when(block == 0)
    def _():
        normed[: low.shape[0]] = low[...]
        normed[low.shape[0] :] = high[...]

    projected = dot(normed[...], weight[...])

    @pl.when(block < q_blocks + k_blocks)
    def _():
        saved[...] = projected
        gain = jnp.where(block < q_blocks, gains[0:1], gains[1:2])
        for first in range(0, projected.shape[1], HD):
            normal = rms_norm(projected[:, first : first + HD])[0] * gain
            turned = pltpu.roll(normal, HD // 2, 1) * sine[...]
            out[:, first : first + HD] = (normal * cosine[...] + turned).astype(bf16)

    @pl.when(block >= q_blocks + k_blocks)
    def _():
        out[...] = projected.astype(bf16)


def project(owner, halves, weight, cosine, sine, gains, into, rows, q_cols, k_cols):
    depth, columns = weight.shape
    own_rows = 2 * halves[1].shape[0]
    step = min(k_cols, 256)
    q_blocks, k_blocks = q_cols // step, k_cols // step
    grid = columns // step
    whole = lambda j, o: (0, 0)
    return pl.pallas_call(
        lambda *refs: project_kernel(q_blocks, k_blocks, *refs),
        out_shape=(
            jax.ShapeDtypeStruct((rows, columns), bf16),
            jax.ShapeDtypeStruct((rows, q_cols + k_cols), f32),
            jax.ShapeDtypeStruct((rows, depth), bf16),
        ),
        grid_spec=pltpu.PrefetchScalarGridSpec(
            num_scalar_prefetch=1,
            grid=(grid,),
            in_specs=[
                pl.BlockSpec((own_rows // 2, depth), whole),
                pl.BlockSpec((own_rows // 2, depth), whole),
                pl.BlockSpec((depth, step), lambda j, o: (0, j)),
                pl.BlockSpec((own_rows, HD), whole),
                pl.BlockSpec((own_rows, HD), whole),
                pl.BlockSpec((2, HD), whole),
            ]
            + [pl.BlockSpec(memory_space=pl.ANY)] * len(into),
            out_specs=(
                pl.BlockSpec((own_rows, step), lambda j, o: (o[0], j)),
                pl.BlockSpec(
                    (own_rows, step),
                    lambda j, o: (o[0], jnp.minimum(j, q_blocks + k_blocks - 1)),
                ),
                pl.BlockSpec((own_rows, depth), lambda j, o: (o[0], 0)),
            ),
        ),
        input_output_aliases={7 + i: i for i in range(len(into))},
        compiler_params=pltpu.CompilerParams(vmem_limit_bytes=VMEM_LIMIT),
        cost_estimate=COST,
    )(owner, *halves, weight, cosine, sine, gains, *into)


def out_kernel(attended, x, weight, gain, hidden_rows, mlp_rows):
    step = pl.program_id(0)
    tile = weight.shape[1]
    here = pl.ds(pl.multiple_of(step * tile, tile), tile)
    hidden_rows[:, here] = x[:, here].astype(f32) + dot(attended[...], weight[...])

    @pl.when(step == pl.num_programs(0) - 1)
    def _():
        mlp_rows[...] = (rms_norm(hidden_rows[...])[0] * gain[...]).astype(bf16)


def out_project(attended, weight, x, gain):
    rows, width = x.shape
    tile = min(512, width)
    full = pl.BlockSpec((rows, width), lambda j: (0, 0))
    return pl.pallas_call(
        out_kernel,
        out_shape=(
            jax.ShapeDtypeStruct((rows, width), f32),
            jax.ShapeDtypeStruct((rows, width), bf16),
        ),
        grid=(width // tile,),
        in_specs=[
            pl.BlockSpec(attended.shape, lambda j: (0, 0)),
            full,
            pl.BlockSpec((weight.shape[0], tile), lambda j: (0, j)),
            pl.BlockSpec((1, width), lambda j: (0, 0)),
        ],
        out_specs=(full, full),
        compiler_params=pltpu.CompilerParams(vmem_limit_bytes=VMEM_LIMIT),
        cost_estimate=COST,
    )(attended, x, weight, gain[None])


def out_back_kernel(count, part, passed, cotangent, hidden_rows, gain, weight, *outs):
    rows_grad, branch, gain_grad, pieces = outs[0], outs[1], outs[2], outs[3:]
    step = pl.program_id(0)

    @pl.when(step == 0)
    def _():
        grad = part[...] + passed[...].astype(f32)
        normal, scale = rms_norm(hidden_rows[...])
        total = cotangent[...].astype(f32) + rms_back(grad, gain[...], normal, scale)
        rows_grad[...] = total
        branch[...] = total.astype(bf16)
        gain_grad[...] = jnp.sum(grad * normal, axis=0, keepdims=True)

    piece = dot(branch[...], weight[...], 1, 1).astype(bf16)
    for k in range(count):

        @pl.when(step == k)
        def _(k=k):
            pieces[k][...] = piece


def out_back(count, part, passed, cotangent, hidden_rows, gain, weight):
    rows, width = part.shape
    cols = weight.shape[0] // count
    full = pl.BlockSpec((rows, width), lambda j: (0, 0))
    line = pl.BlockSpec((1, width), lambda j: (0, 0))
    results = pl.pallas_call(
        lambda *refs: out_back_kernel(count, *refs),
        out_shape=(
            jax.ShapeDtypeStruct((rows, width), f32),
            jax.ShapeDtypeStruct((rows, width), bf16),
            jax.ShapeDtypeStruct((1, width), f32),
        )
        + (jax.ShapeDtypeStruct((rows, cols), bf16),) * count,
        grid=(count,),
        in_specs=[full, full, full, full, line, pl.BlockSpec((cols, width), lambda j: (j, 0))],
        out_specs=(full, full, line) + (pl.BlockSpec((rows, cols), lambda j: (0, 0)),) * count,
        compiler_params=pltpu.CompilerParams(vmem_limit_bytes=VMEM_WHOLE),
        cost_estimate=COST,
    )(part, passed, cotangent, hidden_rows, gain[None], weight)
    return results[0], results[1], results[2][0], list(results[3:])


def feed_kernel(rows_in, low, high, w_gate, w_up, w_down, *refs):
    hidden, grads, all_in, all_cot, part = refs[-5:]
    step = pl.program_id(0)

    @pl.when(step == 0)
    def _():
        all_in[...] = rows_in[...]
        all_cot[: low.shape[0]] = low[...]
        all_cot[low.shape[0] :] = high[...]

    tile = w_gate.shape[1]
    units = grads.shape[1] // 2
    gate_act = dot(rows_in[...], w_gate[...])
    up_act = dot(rows_in[...], w_up[...])
    hidden_grad = dot(all_cot[...], w_down[...])
    sigmoid = jax.nn.sigmoid(gate_act)
    silu = gate_act * sigmoid
    hidden[...] = (silu * up_act).astype(bf16)
    gate_grad = hidden_grad * up_act * sigmoid * (1.0 + gate_act * (1.0 - sigmoid))
    gate_grad = gate_grad.astype(bf16)
    up_grad = (hidden_grad * silu).astype(bf16)
    first = pl.multiple_of(step * tile, tile)
    grads[:, pl.ds(first, tile)] = gate_grad
    grads[:, pl.ds(pl.multiple_of(units + first, tile), tile)] = up_grad
    more = dot(gate_grad, w_gate[...], 1, 1) + dot(up_grad, w_up[...], 1, 1)

    @pl.when(step == 0)
    def _():
        part[...] = more

    @pl.when(step > 0)
    def _():
        part[...] += more


def feed(index, rows_in, halves, weights, into, count):
    rows, width = rows_in.shape
    units = weights.shape[1] // 3
    tile = 512 if units % 512 == 0 else 256
    steps = units // tile
    full = pl.BlockSpec((rows, width), lambda j: (0, 0))
    here = pl.BlockSpec((rows, width), lambda j: (index, 0))
    *into, part = pl.pallas_call(
        feed_kernel,
        out_shape=tuple(
            jax.ShapeDtypeStruct((count * rows, cols), bf16)
            for cols in (units, 2 * units, width, width)
        )
        + (jax.ShapeDtypeStruct((rows, width), f32),),
        grid=(steps,),
        in_specs=[
            full,
            pl.BlockSpec(halves[0].shape, lambda j: (0, 0)),
            pl.BlockSpec(halves[1].shape, lambda j: (0, 0)),
            pl.BlockSpec((width, tile), lambda j: (0, j)),
            pl.BlockSpec((width, tile), lambda j: (0, steps + j)),
            pl.BlockSpec((width, tile), lambda j: (0, 2 * steps + j)),
        ]
        + [pl.BlockSpec(memory_space=pl.ANY)] * len(into),
        out_specs=(
            pl.BlockSpec((rows, tile), lambda j: (index, j)),
            pl.BlockSpec((rows, 2 * units), lambda j: (index, 0)),
            here,
            here,
            full,
        ),
        input_output_aliases={6 + i: i for i in range(len(into))},
        compiler_params=pltpu.CompilerParams(vmem_limit_bytes=VMEM_LIMIT),
        cost_estimate=COST,
    )(rows_in, *halves, weights, weights, weights, *into)
    return tuple(into), part


def weight_grad_kernel(left, right, out):
    out[...] = dot(left[...], right[...], 0, 0).astype(bf16)


def weight_grad(left, right):
    rows, height = left.shape
    width = right.shape[1]
    tile = 512 if width % 512 == 0 else 256
    return pl.pallas_call(
        weight_grad_kernel,
        out_shape=jax.ShapeDtypeStruct((height, width), bf16),
        grid=(width // tile,),
        in_specs=[
            pl.BlockSpec((rows, height), lambda j: (0, 0)),
            pl.BlockSpec((rows, tile), lambda j: (0, j)),
        ],
        out_specs=pl.BlockSpec((height, tile), lambda j: (0, j)),
        compiler_params=pltpu.CompilerParams(vmem_limit_bytes=VMEM_WHOLE),
        cost_estimate=COST,
    )(left, right)


def head_weight_grad_kernel(normed, q_grad, k_grad, v_grad, weight, out, gain):
    first, gain_total = 0, 0.0
    for grad in (q_grad, k_grad, v_grad):
        last = first + grad.shape[1]
        part = dot(normed[...], grad[...], 0, 0)
        out[:, first:last] = part.astype(bf16)
        product = part * weight[:, first:last].astype(f32)
        for column in range(0, last - first, HD):
            gain_total += product[:, column : column + HD]
        first = last
    gain[...] = gain_total


def head_weight_grad(normed, grads, weight):
    rows, width = normed.shape
    columns = weight.shape[1]
    tile = min(512, width)
    return pl.pallas_call(
        head_weight_grad_kernel,
        out_shape=(
            jax.ShapeDtypeStruct((width, columns), bf16),
            jax.ShapeDtypeStruct((width, HD), f32),
        ),
        grid=(width // tile,),
        in_specs=[pl.BlockSpec((rows, tile), lambda j: (0, j))]
        + [pl.BlockSpec(g.shape, lambda j: (0, 0)) for g in grads]
        + [pl.BlockSpec((tile, columns), lambda j: (j, 0))],
        out_specs=(
            pl.BlockSpec((tile, columns), lambda j: (j, 0)),
            pl.BlockSpec((tile, HD), lambda j: (j, 0)),
        ),
        compiler_params=pltpu.CompilerParams(vmem_limit_bytes=VMEM_LIMIT),
        cost_estimate=COST,
    )(normed, *grads, weight)


def down_kernel(hidden, weight, *refs):
    total = dot(hidden[...], weight[...], 1, 1)
    for more in refs[:-1]:
        total += more[...].astype(f32)
    refs[-1][...] = total.astype(refs[-1].dtype)


def down_project(index, hidden, weights, *more, dtype=bf16):
    width, units = weights.shape[0], hidden.shape[1]
    rows = more[0].shape[0] if more else hidden.shape[0] // lax.axis_size("tensor")
    tile = min(512, width)
    block = pl.BlockSpec((rows, tile), lambda j: (0, j))
    return pl.pallas_call(
        down_kernel,
        out_shape=jax.ShapeDtypeStruct((rows, width), dtype),
        grid=(width // tile,),
        in_specs=[
            pl.BlockSpec((rows, units), lambda j: (index, 0)),
            pl.BlockSpec((tile, units), lambda j: (j, 2)),
        ]
        + [block] * len(more),
        out_specs=block,
        compiler_params=pltpu.CompilerParams(vmem_limit_bytes=VMEM_LIMIT),
        cost_estimate=COST,
    )(hidden, weights, *more)


SCORE_SCALE = HD ** (-0.5) * 1.4426950408889634


def split_scores(query, keys, first):
    last = first + query.shape[0]
    beside = dot(query, keys[first:last], 1, 1)
    row = lax.broadcasted_iota(jnp.int32, beside.shape, 0)
    column = lax.broadcasted_iota(jnp.int32, beside.shape, 1)
    beside = jnp.where(row >= column, beside, NEGATIVE)
    parts = [(first, last, beside)]
    if first:
        parts.append((0, first, dot(query, keys[:first], 1, 1)))
    return parts


def attend_kernel(queries, keys, values, out, logs):
    rows = min(QUERY_ROWS, queries.shape[0])
    for first in range(0, queries.shape[0], rows):
        for head in range(queries.shape[1] // HD):
            here = (slice(first, first + rows), slice(head * HD, (head + 1) * HD))
            parts = split_scores(queries[here], keys, first)
            top = None
            for _, _, scores in parts:
                most = jnp.max(scores, axis=1, keepdims=True)
                top = most if top is None else jnp.maximum(top, most)
            total = attended = 0.0
            for start, end, scores in parts:
                exponent = jnp.exp2((scores - top) * SCORE_SCALE)
                total += jnp.sum(exponent, axis=1, keepdims=True)
                attended += dot(exponent.astype(bf16), values[start:end])
            out[here] = (attended * (1.0 / total)).astype(bf16)
            logs[0, here[0], head : head + 1] = top * SCORE_SCALE + jnp.log2(total)


def attend(qkv, length, q_cols, k_cols):
    rows = qkv.shape[0]
    groups = k_cols // HD
    share = q_cols // groups
    return pl.pallas_call(
        attend_kernel,
        out_shape=(
            jax.ShapeDtypeStruct((rows, q_cols), bf16),
            jax.ShapeDtypeStruct((rows // length * groups, length, HD), f32),
        ),
        grid=(rows // length, groups),
        in_specs=[
            pl.BlockSpec((length, share), lambda s, g: (s, g)),
            pl.BlockSpec((length, HD), lambda s, g: (s, q_cols // HD + g)),
            pl.BlockSpec((length, HD), lambda s, g: (s, (q_cols + k_cols) // HD + g)),
        ],
        out_specs=(
            pl.BlockSpec((length, share), lambda s, g: (s, g)),
            pl.BlockSpec((1, length, HD), lambda s, g: (s * groups + g, 0, 0)),
        ),
        compiler_params=pltpu.CompilerParams(vmem_limit_bytes=VMEM_LIMIT),
        cost_estimate=COST,
    )(qkv, qkv, qkv)


def unrope_unnorm(grad, projected, gain, cosine, sine):
    grad = grad * cosine + pltpu.roll(grad * sine, HD // 2, 1)
    normal, scale = rms_norm(projected)
    return rms_back(grad, gain, normal, scale), grad * normal


def attend_back_kernel(
    count, place, queries, keys, values, attended, logs, q_proj, k_proj, cosine, sine, gains, *refs
):
    pieces, (q_out, k_out, v_out, gain_out, grads, key_grad, value_grad) = (
        refs[:count],
        refs[count:],
    )
    length = queries.shape[0]
    size = length // count
    for step, piece in enumerate(pieces):
        owner = lax.rem(place[0] + step, count)
        grads[pl.ds(pl.multiple_of(owner * size, size), size), :] = piece[...]
    rows = min(QUERY_ROWS, length)
    scale = HD ** (-0.5)
    gain_total = jnp.zeros((1, HD), f32)
    for first in range(length - rows, -1, -rows):
        for head in range(queries.shape[1] // HD):
            here = (slice(first, first + rows), slice(head * HD, (head + 1) * HD))
            query, grad = queries[here], grads[here]
            log = logs[0, here[0], head : head + 1]
            delta = jnp.sum(
                grad.astype(f32) * attended[here].astype(f32), axis=1, keepdims=True
            )
            query_grad = 0.0
            for start, end, scores in split_scores(query, keys, first):
                probs = jnp.exp2(scores * SCORE_SCALE - log)
                prob_grad = dot(grad, values[start:end], 1, 1)
                score_grad = (probs * (prob_grad - delta)).astype(bf16)
                value_part = dot(probs.astype(bf16), grad, 0, 0)
                key_part = dot(score_grad, query, 0, 0)
                query_grad += dot(score_grad, keys[start:end])
                if first + rows == length and head == 0:
                    key_grad[start:end] = key_part
                    value_grad[start:end] = value_part
                else:
                    key_grad[start:end] += key_part
                    value_grad[start:end] += value_part
            out, gain_rows = unrope_unnorm(
                query_grad * scale, q_proj[here], gains[0:1], cosine[here[0]], sine[here[0]]
            )
            q_out[here] = out.astype(bf16)
            gain_total += jnp.sum(gain_rows, axis=0, keepdims=True)
    out, gain_rows = unrope_unnorm(
        key_grad[...] * scale, k_proj[...], gains[1:2], cosine[...], sine[...]
    )
    k_out[...] = out.astype(bf16)
    v_out[...] = value_grad[...].astype(bf16)
    gain_out[0, 0:1] = gain_total
    gain_out[0, 1:2] = jnp.sum(gain_rows, axis=0, keepdims=True)


def attend_back(place, qkv, attended, logs, pieces, saved, cosine, sine, gains, q_cols, k_cols):
    rows = qkv.shape[0]
    groups = k_cols // HD
    share = q_cols // groups
    count = len(pieces)
    return pl.pallas_call(
        lambda *refs: attend_back_kernel(count, *refs),
        out_shape=(
            jax.ShapeDtypeStruct((rows, q_cols), bf16),
            jax.ShapeDtypeStruct((rows, k_cols), bf16),
            jax.ShapeDtypeStruct((rows, k_cols), bf16),
            jax.ShapeDtypeStruct((groups, 2, HD), f32),
        ),
        grid_spec=pltpu.PrefetchScalarGridSpec(
            num_scalar_prefetch=1,
            grid=(groups,),
            in_specs=[
                pl.BlockSpec((rows, share), lambda g, p: (0, g)),
                pl.BlockSpec((rows, HD), lambda g, p: (0, q_cols // HD + g)),
                pl.BlockSpec((rows, HD), lambda g, p: (0, (q_cols + k_cols) // HD + g)),
                pl.BlockSpec((rows, share), lambda g, p: (0, g)),
                pl.BlockSpec((1, rows, HD), lambda g, p: (g, 0, 0)),
                pl.BlockSpec((rows, share), lambda g, p: (0, g)),
                pl.BlockSpec((rows, HD), lambda g, p: (0, q_cols // HD + g)),
                pl.BlockSpec((rows, HD), lambda g, p: (0, 0)),
                pl.BlockSpec((rows, HD), lambda g, p: (0, 0)),
                pl.BlockSpec((2, HD), lambda g, p: (0, 0)),
            ]
            + [pl.BlockSpec((rows // count, share), lambda g, p: (0, g))] * count,
            out_specs=(
                pl.BlockSpec((rows, share), lambda g, p: (0, g)),
                pl.BlockSpec((rows, HD), lambda g, p: (0, g)),
                pl.BlockSpec((rows, HD), lambda g, p: (0, g)),
                pl.BlockSpec((1, 2, HD), lambda g, p: (g, 0, 0)),
            ),
            scratch_shapes=[
                pltpu.VMEM((rows, share), bf16),
                pltpu.VMEM((rows, HD), f32),
                pltpu.VMEM((rows, HD), f32),
            ],
        ),
        compiler_params=pltpu.CompilerParams(vmem_limit_bytes=VMEM_WHOLE),
        cost_estimate=COST,
    )(place, qkv, qkv, qkv, attended, logs, saved, saved, cosine, sine, gains, *pieces)


def normed_back_kernel(_, q_grad, k_grad, v_grad, weight, out, grads):
    @pl.when(pl.program_id(0) == 0)
    def _():
        first = 0
        for grad in (q_grad, k_grad, v_grad):
            last = first + grad.shape[1]
            grads[:, first:last] = grad[...]
            first = last

    out[...] = dot(grads[...], weight[...], 1, 1).astype(out.dtype)


def normed_back(owner, grads, weight, own_rows, dtype=f32):
    width, columns = weight.shape
    tile = min(512, width)
    return pl.pallas_call(
        normed_back_kernel,
        out_shape=jax.ShapeDtypeStruct((own_rows, width), dtype),
        grid_spec=pltpu.PrefetchScalarGridSpec(
            num_scalar_prefetch=1,
            grid=(width // tile,),
            in_specs=[pl.BlockSpec((own_rows, g.shape[1]), lambda j, o: (o[0], 0)) for g in grads]
            + [pl.BlockSpec((tile, columns), lambda j, o: (j, 0))],
            out_specs=pl.BlockSpec((own_rows, tile), lambda j, o: (0, j)),
            scratch_shapes=[pltpu.VMEM((own_rows, columns), bf16)],
        ),
        compiler_params=pltpu.CompilerParams(vmem_limit_bytes=VMEM_WHOLE),
        cost_estimate=COST,
    )(owner, *grads, weight)


def per_device(
    tokens,
    positions,
    attn_gain,
    query_weight,
    key_weight,
    value_weight,
    query_gain,
    key_gain,
    out_weight,
    mlp_gain,
    gate_weight,
    up_weight,
    down_weight,
    cotangent,
):
    own_rows, width = tokens.shape
    count = lax.axis_size("tensor")
    place = lax.axis_index("tensor")
    assert count * own_rows == LEN
    q_cols, k_cols = query_weight.shape[1], key_weight.shape[1]
    own_width = query_weight.shape[0]
    rows_size = own_rows * width
    units = gate_weight.shape[1]
    owners = lax.rem(place - jnp.arange(count, dtype=jnp.int32) + count, count)

    x_rows = tokens.astype(f32)
    x_normal, x_scale = rms_norm(x_rows)
    digits = jnp.stack([positions // 128, positions % 128]).astype(bf16).reshape(-1)
    head_cols, out_cols = out_weight.shape
    digit_lines = -(-digits.size // (16 * out_cols)) * 16
    digits = jnp.pad(digits, (0, digit_lines * out_cols - digits.size)).reshape(-1, out_cols)
    out_lines = jnp.concatenate([out_weight, digits], axis=0)
    normed_rows = (x_normal * attn_gain).astype(bf16)
    middle = own_rows // 2
    lows, highs = [normed_rows[:middle]], [normed_rows[middle:]]

    heads_weight = after((query_weight, key_weight, value_weight), lows, highs)
    w_qkv = lax.all_gather(jnp.concatenate(heads_weight, axis=1), "dp", axis=0, tiled=True)
    out_rows = [out_lines]
    for step in range(1, count):
        pairs = [(i, (i + step) % count) for i in range(count)]
        out_rows.append(lax.ppermute(out_lines, "tensor", pairs))
    lows.append(pass_on(lows[-1], "tensor"))
    highs.append(pass_on(highs[-1], "tensor"))
    w_feed = after((gate_weight, up_weight, down_weight), out_rows[1])
    w_feed = jnp.concatenate([w_feed[0], w_feed[1], w_feed[2].T], axis=1)
    lows, highs, out_rows, w_feed = fence(lows, highs, out_rows, w_feed)
    w_out = jnp.concatenate([lines[:head_cols] for lines in out_rows], axis=0)
    w_out, w_feed = fence(w_out, w_feed)
    w_out = lax.all_gather(w_out, "dp", axis=1, tiled=True)

    group_rows = count * own_rows
    into = ()
    head_gains = jnp.stack([query_gain, key_gain])
    tables = []

    def project_block(step, into):
        digit_rows = out_rows[step][head_cols:].reshape(-1)[: 2 * own_rows]
        digit_rows = digit_rows.reshape(2, own_rows).astype(f32)
        tables.append(angle_tables(digit_rows[0] * 128.0 + digit_rows[1], HD))
        return project(
            owners[step : step + 1],
            (lows[step], highs[step]),
            w_qkv,
            *tables[-1],
            head_gains,
            into,
            group_rows,
            q_cols,
            k_cols,
        )

    for step in range(2, count):
        lows.append(pass_on(lows[-1], "tensor"))
        highs.append(pass_on(highs[-1], "tensor"))
        for block in range(0 if step == 2 else step - 1, step):
            into = project_block(block, into)
        lows[step], highs[step], into = fence(lows[step], highs[step], into)
        if step == 2:
            w_feed = lax.all_gather(after(w_feed, into), "dp", axis=0, tiled=True)
    split = own_rows * 3 // 4
    cot_low, cot_high = after((cotangent[:split], cotangent[split:]), lows[-1], highs[-1])
    cot_lows, cot_highs = [cot_low], [cot_high]
    cot_lows.append(pass_on(cot_low, "tensor"))
    into = project_block(count - 1, into)
    qkv, saved, normed = into
    cosine = in_order([pair[0] for pair in tables], "tensor", -1)
    sine = in_order([pair[1] for pair in tables], "tensor", -1)
    attended_heads, logs = attend(qkv, LEN, q_cols, k_cols)
    attended_heads, cot_lows = fence(attended_heads, cot_lows)

    pieces = [rows_of(attended_heads, place, own_rows)]
    for step in range(1, count):
        piece = rows_of(attended_heads, lax.rem(place + step, count), own_rows)
        pieces.append(lax.ppermute(piece, "tensor", [(i, (i + step) % count) for i in range(count)]))
    pieces, cot_lows, cot_highs = fence(pieces, cot_lows, cot_highs)
    attended = jnp.concatenate(pieces, axis=1)
    cot_highs.append(pass_on(cot_highs[-1], "tensor"))
    hidden_rows, mlp_rows = out_project(attended, w_out, tokens, mlp_gain)

    into = ()
    ins, parts = [mlp_rows], []
    grad_sum = mixed_sum = None
    mixed_parts = []
    for step in range(count + 2):
        if step + 1 < count:
            ins.append(pass_on(ins[-1], "tensor"))
        if step and len(cot_highs) < count:
            cot_highs.append(pass_on(cot_highs[-1], "tensor"))
        if len(cot_lows) < count:
            cot_lows.append(pass_on(cot_lows[-1], "tensor"))
        if step > 2:
            send = parts[step - 2]
            if step > 3:
                send = send + grad_sum.astype(f32)
            grad_sum = pass_on(send.astype(bf16), "tensor")
        if 2 < step <= count:
            send = mixed_parts[step - 3]
            if step > 3:
                send = send + mixed_sum.astype(f32)
            mixed_sum = pass_on(send.astype(bf16), "tensor")
        for block in {0: [], 1: [0, 1], count: [], count + 1: []}.get(step, [step]):
            into, part = feed(
                block, ins[block], (cot_lows[block], cot_highs[block]), w_feed, into, count
            )
            parts.append(part)
        if step in (1, 2) or 3 < step <= count:
            mixed_parts.append(
                down_project(step if step < 3 else step - 1, into[0], w_feed, dtype=f32)
            )
        if step == count - 1:
            gate_up_wgrad = weight_grad(into[2], into[1])
            down_wgrad = weight_grad(into[3], into[0])
            into, gate_up_wgrad, down_wgrad = fence(into, gate_up_wgrad, down_wgrad)
        ins, cot_lows, cot_highs, into, parts, grad_sum, mixed_sum, mixed_parts = fence(
            ins, cot_lows, cot_highs, into, parts, grad_sum, mixed_sum, mixed_parts
        )
        if step == count - 1:
            gate_up_wgrad = after(gate_up_wgrad, into)
            gate_up_sum = lax.psum_scatter(gate_up_wgrad, "dp", scatter_dimension=0, tiled=True)

    send = (mixed_parts[-1] + mixed_sum.astype(f32)).astype(bf16)
    last_low = pass_on(send[:middle], "tensor")
    rows_grad, branch_grad, mlp_gain_part, pieces = out_back(
        count, parts[0], grad_sum, cotangent, hidden_rows, mlp_gain, w_out
    )
    pieces, branch_grad, last_low, send = fence(pieces, branch_grad, last_low, send)

    for step in range(1, count):
        pieces[step] = lax.ppermute(
            pieces[step], "tensor", [(i, (i - step) % count) for i in range(count)]
        )
    out_wgrad = weight_grad(branch_grad, attended)
    pieces, out_wgrad, send = fence(pieces, out_wgrad, send)
    out_block = lax.psum_scatter(out_wgrad, "dp", scatter_dimension=0, tiled=True)

    last_high = pass_on(send[middle:], "tensor")
    *head_grads, gain_parts = attend_back(
        place.reshape(1),
        qkv,
        attended_heads,
        logs,
        pieces,
        saved,
        cosine,
        sine,
        head_gains,
        q_cols,
        k_cols,
    )
    head_grads, gain_parts, last_high = fence(head_grads, gain_parts, last_high)
    mixed_sum = jnp.concatenate([last_low, last_high], axis=0)
    first_part = normed_back(owners[1:2], head_grads, w_qkv, own_rows, bf16)
    normed_sum = pass_on(first_part, "tensor")

    head_grads = after(head_grads, first_part)
    part = normed_back(owners[2 % count :][:1], head_grads, w_qkv, own_rows)
    qkv_wgrad, attn_gain_part = head_weight_grad(normed, head_grads, w_qkv)
    gains = jnp.concatenate(
        [
            jnp.sum(attn_gain_part, axis=1) / attn_gain,
            mlp_gain_part,
            jnp.sum(gain_parts, axis=0).reshape(-1),
        ]
    )
    beside_cols = -(-gains.size // (own_width // 2 * HD)) * HD
    beside = jnp.pad(gains, (0, own_width * beside_cols - gains.size))
    beside = beside.reshape(own_width, beside_cols).astype(bf16)
    qkv_sum = HalvingSum(qkv_wgrad, "dp", beside).prepare().launch(rows_size // 2)
    normed_sum, part, qkv_sum.state, gate_up_sum = fence(
        normed_sum, part, qkv_sum.state, gate_up_sum
    )
    down_wgrad = after(down_wgrad, normed_sum)
    down_sum = lax.psum_scatter(down_wgrad, "dp", scatter_dimension=0, tiled=True)
    out_pieces = []
    for step in range(2, count):
        send = (part + normed_sum.astype(f32)).astype(bf16)
        normed_sum = pass_on(send, "tensor")
        qkv_sum.state, head_grads = fence(qkv_sum.state, head_grads, send)[:2]
        if qkv_sum.steps < qkv_sum.bits:
            qkv_sum.prepare().launch(rows_size)
        if step == 2:
            mixed = down_project(0, into[0], w_feed, mixed_sum, hidden_rows)
        if step == count - 1:
            out_block = after(out_block, send)
            out_pieces = [out_block[:, s * head_cols : (s + 1) * head_cols] for s in range(count)]
            gate_sum = gate_up_sum[:, :units].astype(f32)
            up_sum = gate_up_sum[:, units:].astype(f32)
        part = normed_back(owners[(step + 1) % count :][:1], head_grads, w_qkv, own_rows)
        if step == count - 1:
            qkv_total = qkv_sum.total(f32)
            normed_sum, part, qkv_total, out_pieces, mixed = fence(
                normed_sum, part, qkv_total, out_pieces, mixed
            )
        else:
            normed_sum, part, qkv_sum.state, out_pieces, mixed = fence(
                normed_sum, part, qkv_sum.state, out_pieces, mixed
            )

    for other in range(1, count):
        pairs = [(i, (i - other) % count) for i in range(count)]
        out_pieces[other] = lax.ppermute(out_pieces[other], "tensor", pairs)
    out_total = sum(piece.astype(f32) for piece in out_pieces).T
    gains = qkv_total[:, q_cols + 2 * k_cols :].reshape(-1)[: gains.size]
    gains = after(gains.reshape(-1, HD), out_pieces[1])
    gains = butterfly_sum(gains, "tensor").reshape(-1)
    normed_grad = part + normed_sum.astype(f32)
    token_grad = (rows_grad + rms_back(normed_grad, attn_gain, x_normal, x_scale)).astype(bf16)
    return (
        mixed,
        token_grad,
        gains[:width],
        qkv_total[:, :q_cols],
        qkv_total[:, q_cols : q_cols + k_cols],
        qkv_total[:, q_cols + k_cols : q_cols + 2 * k_cols],
        gains[2 * width : 2 * width + HD],
        gains[2 * width + HD : 2 * width + 2 * HD],
        out_total,
        gains[width : 2 * width],
        gate_sum,
        up_sum,
        down_sum.astype(f32).T,
    )


def solution(mesh):
    in_specs = (
        P(("dp", "tensor"), None),
        P(("dp", "tensor")),
        P(),
        P("dp", "tensor"),
        P("dp", "tensor"),
        P("dp", "tensor"),
        P(),
        P(),
        P("tensor", "dp"),
        P(),
        P("dp", "tensor"),
        P("dp", "tensor"),
        P("tensor", "dp"),
        P(("dp", "tensor"), None),
    )
    out_specs = (
        P(("dp", "tensor"), None),
        P(("dp", "tensor"), None),
        P(),
        P("dp", "tensor"),
        P("dp", "tensor"),
        P("dp", "tensor"),
        P(),
        P(),
        P("tensor", "dp"),
        P(),
        P("dp", "tensor"),
        P("dp", "tensor"),
        P("tensor", "dp"),
    )
    return jax.shard_map(
        per_device, mesh=mesh, in_specs=in_specs, out_specs=out_specs, check_vma=False
    )
```

```python
import jax
import jax.numpy as jnp
from jax import lax
from jax.experimental import pallas as pl
from jax.experimental.pallas import tpu as pltpu
from jax.sharding import PartitionSpec as P

HD = 128
LEN = 1024

EPSILON = 1e-06
NEGATIVE = -1e30

f32 = jnp.float32
bf16 = jnp.bfloat16


def rms_norm(vector):
    scale = lax.rsqrt(jnp.mean(vector * vector, axis=-1, keepdims=True) + EPSILON)
    return vector * scale, scale


def rms_back(grad, gains, normal, scale):
    weighted = grad * gains
    return scale * (weighted - normal * jnp.mean(weighted * normal, axis=-1, keepdims=True))


def angle_tables(places, width):
    frequency = 1000000.0 ** (-jnp.arange(0, width, 2, dtype=f32) / width)
    angles = places.astype(f32)[:, None] * frequency[None, :]
    cosine, sine = jnp.cos(angles), jnp.sin(angles)
    return (
        jnp.concatenate([cosine, cosine], axis=-1),
        jnp.concatenate([-sine, sine], axis=-1),
    )


def contract(left, right, left_dim, right_dim):
    return lax.dot_general(
        left, right, (((left_dim,), (right_dim,)), ((), ())), preferred_element_type=f32
    )


def fence(*trees):
    leaves, shape = jax.tree.flatten(trees)
    return jax.tree.unflatten(shape, lax.optimization_barrier(leaves))


def after(value, *others):
    return fence(value, others)[0]


def pass_on(value, axis):
    count = lax.axis_size(axis)
    return lax.ppermute(value, axis, [(i, (i + 1) % count) for i in range(count)])


def sum_kernel(count, columns, _, *refs):
    total = refs[0][:, :, :columns].astype(f32)
    for more in refs[1:count]:
        total += more[:, :, :columns].astype(f32)
    out = refs[-1]
    out[:, :, :columns] = total.astype(out.dtype)
    if len(refs) > count + 1:
        total = refs[count][...].astype(f32)
        for more in refs[1:count]:
            total += more[:, :, columns:].astype(f32)
        out[:, :, columns:] = total.astype(out.dtype)


def sum_blocks(places, arrays, half, rows, dtype, beside=None):
    size, columns = len(places[0]), arrays[0].shape[2]
    flat = jnp.stack([jnp.asarray(p, jnp.int32) for line in places for p in line])
    total = columns + (beside.shape[2] if beside is not None else 0)

    def spec(i):
        whole = arrays[i].shape[1] == rows
        return pl.BlockSpec(
            (1, rows, arrays[i].shape[2]),
            lambda k, at: (at[i * size + k], 0 if whole else half, 0),
        )

    specs = [spec(i) for i in range(len(arrays))]
    if beside is not None:
        whole = beside.shape[1] == rows
        specs.append(
            pl.BlockSpec(
                (1, rows, beside.shape[2]), lambda k, at: (0, 0 if whole else half, 0)
            )
        )
        arrays = list(arrays) + [beside]
    return pl.pallas_call(
        lambda *refs: sum_kernel(len(places), columns, *refs),
        out_shape=jax.ShapeDtypeStruct((size, rows, total), dtype),
        grid_spec=pltpu.PrefetchScalarGridSpec(
            num_scalar_prefetch=1,
            grid=(size,),
            in_specs=specs,
            out_specs=pl.BlockSpec((1, rows, total), lambda k, at: (k, 0, 0)),
        ),
        compiler_params=pltpu.CompilerParams(vmem_limit_bytes=VMEM_LIMIT),
        cost_estimate=COST,
    )(flat, *arrays)


class HalvingSum:
    def __init__(self, blocks, axis, beside=None):
        self.axis, self.count = axis, lax.axis_size(axis)
        self.bits = self.count.bit_length() - 1
        assert self.count == 1 << self.bits
        self.rows = blocks.shape[0] // self.count
        self.beside = None if beside is None else beside[None]
        others = list(range(1, self.bits))
        self.orders = ([0] + others, [0] + others[::-1])
        self.state = (blocks.reshape((self.count, self.rows) + blocks.shape[1:]), [])
        self.steps = 0

    def mine(self, bit):
        return lax.rem(lax.div(lax.axis_index(self.axis), 1 << bit), 2)

    def addends(self, half, step, sent):
        order = self.orders[half]
        free = sorted(order[step + 1 :]) if sent else []
        blocks = []
        for number in range(1 << len(free)):
            value = {bit: (number >> rank) & 1 for rank, bit in enumerate(free)}
            for bit in order:
                if bit not in value:
                    value[bit] = self.mine(bit)
            if sent:
                value[order[step]] = 1 - value[order[step]]
            blocks.append(value)
        arrays = [(self.state[0], sorted(order))]
        for before, arrived in enumerate(self.state[1]):
            pieces = arrived[min(half, len(arrived) - 1)]
            pieces = pieces[0] if len(pieces) == 1 else jnp.concatenate(pieces, axis=0)
            arrays.append((pieces, sorted(order[before + 1 :])))
        places = [
            [sum((v[bit] << rank for rank, bit in enumerate(bits)), jnp.int32(0)) for v in blocks]
            for _, bits in arrays
        ]
        return places, [array for array, _ in arrays]

    def prepare(self):
        first = self.steps == 0
        self.sends = []
        for half in range(1 if first else 2):
            places, arrays = self.addends(half, self.steps, True)
            rows = self.rows if first else self.rows // 2
            self.sends.append(sum_blocks(places, arrays, half, rows, bf16, self.beside))
        return self

    def launch(self, piece_size):
        arrived = []
        for half, send in enumerate(self.sends):
            bit = self.orders[half][self.steps]
            pairs = [(i, i ^ (1 << bit)) for i in range(self.count)]
            parts = max(1, send.size // piece_size)
            pieces = jnp.split(send, parts) if send.shape[0] % parts == 0 else [send]
            arrived.append([lax.ppermute(piece, self.axis, pairs) for piece in pieces])
        self.state = (self.state[0], self.state[1] + [arrived])
        self.steps += 1
        return self

    def step(self):
        return self if self.steps == self.bits else self.prepare().launch(self.state[0].size)

    def total(self, dtype):
        while self.steps < self.bits:
            self.step()
        halves = []
        for half in range(2):
            places, arrays = self.addends(half, self.bits, False)
            halves.append(sum_blocks(places, arrays, half, self.rows // 2, dtype, self.beside)[0])
        return jnp.concatenate(halves, axis=0)


def butterfly_sum(value, axis):
    count = lax.axis_size(axis)
    assert count & (count - 1) == 0
    bit = 1
    while bit < count:
        value = value + lax.ppermute(value, axis, [(i, i ^ bit) for i in range(count)])
        bit *= 2
    return value


def rows_of(array, index, rows):
    return lax.dynamic_slice_in_dim(array, index * rows, rows, axis=0)


def in_order(blocks, axis, sign, dim=0):
    count = lax.axis_size(axis)
    place = lax.axis_index(axis)
    size = blocks[0].shape[dim]
    shape = list(blocks[0].shape)
    shape[dim] *= count
    whole = jnp.zeros(shape, blocks[0].dtype)
    for step, block in enumerate(blocks):
        owner = lax.rem(place + sign * step + count, count)
        whole = lax.dynamic_update_slice_in_dim(whole, block, owner * size, axis=dim)
    return whole


VMEM_LIMIT = 48 * 2**20
VMEM_WHOLE = 60 * 2**20
COST = pl.CostEstimate(flops=2**20, bytes_accessed=2**20, transcendentals=0)
QUERY_ROWS = 256


def dot(left, right, left_dim=1, right_dim=0):
    return contract(left, right, left_dim, right_dim)


def project_kernel(q_heads, k_heads, _, low, high, weight, cosine, sine, gains, *refs):
    out, saved, normed = refs[-3:]
    block = pl.program_id(0)

    @pl.when(block == 0)
    def _():
        normed[: low.shape[0]] = low[...]
        normed[low.shape[0] :] = high[...]

    projected = dot(normed[...], weight[...])
    saved[...] = projected

    def rotated(head, gain):
        normal = rms_norm(projected[:, head * HD : (head + 1) * HD])[0] * gain
        turned = pltpu.roll(normal, HD // 2, 1) * sine[...]
        return (normal * cosine[...] + turned).astype(bf16)

    @pl.when(block == 0)
    def _():
        for head in range(q_heads):
            out[:, head * HD : (head + 1) * HD] = rotated(head, gains[0:1])

    @pl.when(block == 1)
    def _():
        for head in range(k_heads):
            out[:, head * HD : (head + 1) * HD] = rotated(head, gains[1:2])
        out[:, k_heads * HD :] = projected[:, k_heads * HD :].astype(bf16)


def project(owner, halves, weight, cosine, sine, gains, into, rows, q_cols, k_cols):
    depth, columns = weight.shape
    own_rows = 2 * halves[1].shape[0]
    assert q_cols == 2 * k_cols
    whole = lambda j, o: (0, 0)
    return pl.pallas_call(
        lambda *refs: project_kernel(q_cols // HD, k_cols // HD, *refs),
        out_shape=(
            jax.ShapeDtypeStruct((rows, columns), bf16),
            jax.ShapeDtypeStruct((rows, columns), f32),
            jax.ShapeDtypeStruct((rows, depth), bf16),
        ),
        grid_spec=pltpu.PrefetchScalarGridSpec(
            num_scalar_prefetch=1,
            grid=(2,),
            in_specs=[
                pl.BlockSpec((own_rows // 2, depth), whole),
                pl.BlockSpec((own_rows // 2, depth), whole),
                pl.BlockSpec((depth, q_cols), lambda j, o: (0, j)),
                pl.BlockSpec((own_rows, HD), whole),
                pl.BlockSpec((own_rows, HD), whole),
                pl.BlockSpec((2, HD), whole),
            ]
            + [pl.BlockSpec(memory_space=pl.ANY)] * len(into),
            out_specs=(
                pl.BlockSpec((own_rows, q_cols), lambda j, o: (o[0], j)),
                pl.BlockSpec((own_rows, q_cols), lambda j, o: (o[0], j)),
                pl.BlockSpec((own_rows, depth), lambda j, o: (o[0], 0)),
            ),
        ),
        input_output_aliases={7 + i: i for i in range(len(into))},
        compiler_params=pltpu.CompilerParams(vmem_limit_bytes=VMEM_LIMIT),
        cost_estimate=COST,
    )(owner, *halves, weight, cosine, sine, gains, *into)


def out_kernel(attended, x, weight, gain, hidden_rows, mlp_rows):
    step = pl.program_id(0)
    tile = weight.shape[1]
    here = pl.ds(pl.multiple_of(step * tile, tile), tile)
    hidden_rows[:, here] = x[:, here].astype(f32) + dot(attended[...], weight[...])

    @pl.when(step == pl.num_programs(0) - 1)
    def _():
        mlp_rows[...] = (rms_norm(hidden_rows[...])[0] * gain[...]).astype(bf16)


def out_project(attended, weight, x, gain):
    rows, width = x.shape
    tile = min(1024, width)
    full = pl.BlockSpec((rows, width), lambda j: (0, 0))
    return pl.pallas_call(
        out_kernel,
        out_shape=(
            jax.ShapeDtypeStruct((rows, width), f32),
            jax.ShapeDtypeStruct((rows, width), bf16),
        ),
        grid=(width // tile,),
        in_specs=[
            pl.BlockSpec(attended.shape, lambda j: (0, 0)),
            full,
            pl.BlockSpec((weight.shape[0], tile), lambda j: (0, j)),
            pl.BlockSpec((1, width), lambda j: (0, 0)),
        ],
        out_specs=(full, full),
        compiler_params=pltpu.CompilerParams(vmem_limit_bytes=VMEM_LIMIT),
        cost_estimate=COST,
    )(attended, x, weight, gain[None])


def out_back_kernel(count, part, passed, cotangent, hidden_rows, gain, weight, *outs):
    rows_grad, branch, gain_grad, pieces = outs[0], outs[1], outs[2], outs[3:]
    step = pl.program_id(0)

    @pl.when(step == 0)
    def _():
        grad = part[...] + passed[...].astype(f32)
        normal, scale = rms_norm(hidden_rows[...])
        total = cotangent[...].astype(f32) + rms_back(grad, gain[...], normal, scale)
        rows_grad[...] = total
        branch[...] = total.astype(bf16)
        gain_grad[...] = jnp.sum(grad * normal, axis=0, keepdims=True)

    both = dot(branch[...], weight[...], 1, 1).astype(bf16)
    cols = pieces[0].shape[1]
    each = weight.shape[0] // cols
    for k in range(count):

        @pl.when(step == k // each)
        def _(k=k):
            pieces[k][...] = both[:, k % each * cols : (k % each + 1) * cols]


def out_back(count, part, passed, cotangent, hidden_rows, gain, weight):
    rows, width = part.shape
    cols = weight.shape[0] // count
    each = 2 - count % 2
    full = pl.BlockSpec((rows, width), lambda j: (0, 0))
    line = pl.BlockSpec((1, width), lambda j: (0, 0))
    results = pl.pallas_call(
        lambda *refs: out_back_kernel(count, *refs),
        out_shape=(
            jax.ShapeDtypeStruct((rows, width), f32),
            jax.ShapeDtypeStruct((rows, width), bf16),
            jax.ShapeDtypeStruct((1, width), f32),
        )
        + (jax.ShapeDtypeStruct((rows, cols), bf16),) * count,
        grid=(count // each,),
        in_specs=[full, full, full, full, line, pl.BlockSpec((each * cols, width), lambda j: (j, 0))],
        out_specs=(full, full, line) + (pl.BlockSpec((rows, cols), lambda j: (0, 0)),) * count,
        compiler_params=pltpu.CompilerParams(vmem_limit_bytes=VMEM_WHOLE),
        cost_estimate=COST,
    )(part, passed, cotangent, hidden_rows, gain[None], weight)
    return results[0], results[1], results[2][0], list(results[3:])


def feed_kernel(rows_in, low, high, w_gate, w_up, w_down, *refs):
    hidden, grads, all_in, all_cot, part = refs[-5:]
    step = pl.program_id(0)

    @pl.when(step == 0)
    def _():
        all_in[...] = rows_in[...]
        all_cot[: low.shape[0]] = low[...]
        all_cot[low.shape[0] :] = high[...]

    tile = w_gate.shape[1]
    units = grads.shape[1] // 2
    gate_act = dot(rows_in[...], w_gate[...])
    up_act = dot(rows_in[...], w_up[...])
    hidden_grad = dot(all_cot[...], w_down[...])
    sigmoid = jax.nn.sigmoid(gate_act)
    silu = gate_act * sigmoid
    hidden[...] = (silu * up_act).astype(bf16)
    gate_grad = hidden_grad * up_act * sigmoid * (1.0 + gate_act * (1.0 - sigmoid))
    gate_grad = gate_grad.astype(bf16)
    up_grad = (hidden_grad * silu).astype(bf16)
    first = pl.multiple_of(step * tile, tile)
    grads[:, pl.ds(first, tile)] = gate_grad
    grads[:, pl.ds(pl.multiple_of(units + first, tile), tile)] = up_grad
    more = dot(gate_grad, w_gate[...], 1, 1) + dot(up_grad, w_up[...], 1, 1)

    @pl.when(step == 0)
    def _():
        part[...] = more

    @pl.when(step > 0)
    def _():
        part[...] += more


def feed(index, rows_in, halves, weights, into, count):
    rows, width = rows_in.shape
    units = weights.shape[1] // 3
    tile = 512 if units % 512 == 0 else 256
    steps = units // tile
    full = pl.BlockSpec((rows, width), lambda j: (0, 0))
    here = pl.BlockSpec((rows, width), lambda j: (index, 0))
    *into, part = pl.pallas_call(
        feed_kernel,
        out_shape=tuple(
            jax.ShapeDtypeStruct((count * rows, cols), bf16)
            for cols in (units, 2 * units, width, width)
        )
        + (jax.ShapeDtypeStruct((rows, width), f32),),
        grid=(steps,),
        in_specs=[
            full,
            pl.BlockSpec(halves[0].shape, lambda j: (0, 0)),
            pl.BlockSpec(halves[1].shape, lambda j: (0, 0)),
            pl.BlockSpec((width, tile), lambda j: (0, j)),
            pl.BlockSpec((width, tile), lambda j: (0, steps + j)),
            pl.BlockSpec((width, tile), lambda j: (0, 2 * steps + j)),
        ]
        + [pl.BlockSpec(memory_space=pl.ANY)] * len(into),
        out_specs=(
            pl.BlockSpec((rows, tile), lambda j: (index, j)),
            pl.BlockSpec((rows, 2 * units), lambda j: (index, 0)),
            here,
            here,
            full,
        ),
        input_output_aliases={6 + i: i for i in range(len(into))},
        compiler_params=pltpu.CompilerParams(vmem_limit_bytes=VMEM_LIMIT),
        cost_estimate=COST,
    )(rows_in, *halves, weights, weights, weights, *into)
    return tuple(into), part


def weight_grad_kernel(left, right, out):
    out[...] = dot(left[...], right[...], 0, 0).astype(bf16)


def weight_grad(left, right):
    rows, height = left.shape
    width = right.shape[1]
    tile = 512 if width % 512 == 0 else 256
    return pl.pallas_call(
        weight_grad_kernel,
        out_shape=jax.ShapeDtypeStruct((height, width), bf16),
        grid=(width // tile,),
        in_specs=[
            pl.BlockSpec((rows, height), lambda j: (0, 0)),
            pl.BlockSpec((rows, tile), lambda j: (0, j)),
        ],
        out_specs=pl.BlockSpec((height, tile), lambda j: (0, j)),
        compiler_params=pltpu.CompilerParams(vmem_limit_bytes=VMEM_WHOLE),
        cost_estimate=COST,
    )(left, right)


def head_weight_grad_kernel(normed, q_grad, k_grad, v_grad, weight, out, gain):
    first, gain_total = 0, 0.0
    for grad in (q_grad, k_grad, v_grad):
        last = first + grad.shape[1]
        part = dot(normed[...], grad[...], 0, 0)
        out[:, first:last] = part.astype(bf16)
        product = part * weight[:, first:last].astype(f32)
        for column in range(0, last - first, HD):
            gain_total += product[:, column : column + HD]
        first = last
    gain[...] = gain_total


def head_weight_grad(normed, grads, weight):
    rows, width = normed.shape
    columns = weight.shape[1]
    tile = min(1024, width)
    return pl.pallas_call(
        head_weight_grad_kernel,
        out_shape=(
            jax.ShapeDtypeStruct((width, columns), bf16),
            jax.ShapeDtypeStruct((width, HD), f32),
        ),
        grid=(width // tile,),
        in_specs=[pl.BlockSpec((rows, tile), lambda j: (0, j))]
        + [pl.BlockSpec(g.shape, lambda j: (0, 0)) for g in grads]
        + [pl.BlockSpec((tile, columns), lambda j: (j, 0))],
        out_specs=(
            pl.BlockSpec((tile, columns), lambda j: (j, 0)),
            pl.BlockSpec((tile, HD), lambda j: (j, 0)),
        ),
        compiler_params=pltpu.CompilerParams(vmem_limit_bytes=VMEM_LIMIT),
        cost_estimate=COST,
    )(normed, *grads, weight)


def down_kernel(hidden, weight, *refs):
    total = dot(hidden[...], weight[...], 1, 1)
    for more in refs[:-1]:
        total += more[...].astype(f32)
    refs[-1][...] = total.astype(refs[-1].dtype)


def down_project(index, hidden, weights, *more, dtype=bf16):
    width, units = weights.shape[0], hidden.shape[1]
    rows = more[0].shape[0] if more else hidden.shape[0] // lax.axis_size("tensor")
    tile = min(1024, width)
    block = pl.BlockSpec((rows, tile), lambda j: (0, j))
    return pl.pallas_call(
        down_kernel,
        out_shape=jax.ShapeDtypeStruct((rows, width), dtype),
        grid=(width // tile,),
        in_specs=[
            pl.BlockSpec((rows, units), lambda j: (index, 0)),
            pl.BlockSpec((tile, units), lambda j: (j, 2)),
        ]
        + [block] * len(more),
        out_specs=block,
        compiler_params=pltpu.CompilerParams(vmem_limit_bytes=VMEM_LIMIT),
        cost_estimate=COST,
    )(hidden, weights, *more)


SCORE_SCALE = HD ** (-0.5) * 1.4426950408889634


def split_scores(query, keys, first):
    last = first + query.shape[0]
    beside = dot(query, keys[first:last], 1, 1)
    row = lax.broadcasted_iota(jnp.int32, beside.shape, 0)
    column = lax.broadcasted_iota(jnp.int32, beside.shape, 1)
    beside = jnp.where(row >= column, beside, NEGATIVE)
    parts = [(first, last, beside)]
    if first:
        parts.append((0, first, dot(query, keys[:first], 1, 1)))
    return parts


def attend_kernel(queries, keys, values, out, logs):
    rows = min(QUERY_ROWS, queries.shape[0])
    for first in range(0, queries.shape[0], rows):
        for head in range(queries.shape[1] // HD):
            here = (slice(first, first + rows), slice(head * HD, (head + 1) * HD))
            parts = split_scores(queries[here], keys, first)
            top = None
            for _, _, scores in parts:
                most = jnp.max(scores, axis=1, keepdims=True)
                top = most if top is None else jnp.maximum(top, most)
            total = attended = 0.0
            for start, end, scores in parts:
                exponent = jnp.exp2((scores - top) * SCORE_SCALE)
                total += jnp.sum(exponent, axis=1, keepdims=True)
                attended += dot(exponent.astype(bf16), values[start:end])
            out[here] = (attended * (1.0 / total)).astype(bf16)
            logs[0, here[0], head : head + 1] = top * SCORE_SCALE + jnp.log2(total)


def attend(qkv, length, q_cols, k_cols):
    rows = qkv.shape[0]
    groups = k_cols // HD
    share = q_cols // groups
    return pl.pallas_call(
        attend_kernel,
        out_shape=(
            jax.ShapeDtypeStruct((rows, q_cols), bf16),
            jax.ShapeDtypeStruct((rows // length * groups, length, HD), f32),
        ),
        grid=(rows // length, groups),
        in_specs=[
            pl.BlockSpec((length, share), lambda s, g: (s, g)),
            pl.BlockSpec((length, HD), lambda s, g: (s, q_cols // HD + g)),
            pl.BlockSpec((length, HD), lambda s, g: (s, (q_cols + k_cols) // HD + g)),
        ],
        out_specs=(
            pl.BlockSpec((length, share), lambda s, g: (s, g)),
            pl.BlockSpec((1, length, HD), lambda s, g: (s * groups + g, 0, 0)),
        ),
        compiler_params=pltpu.CompilerParams(vmem_limit_bytes=VMEM_LIMIT),
        cost_estimate=COST,
    )(qkv, qkv, qkv)


def unrope_unnorm(grad, projected, gain, cosine, sine):
    grad = grad * cosine + pltpu.roll(grad * sine, HD // 2, 1)
    normal, scale = rms_norm(projected)
    return rms_back(grad, gain, normal, scale), grad * normal


def attend_back_kernel(
    count, place, queries, keys, values, logs, q_proj, k_proj, cosine, sine, gains, *refs
):
    pieces, (q_out, k_out, v_out, gain_out, grads, key_grad, value_grad) = (
        refs[:count],
        refs[count:],
    )
    length = queries.shape[0]
    size = length // count
    for step, piece in enumerate(pieces):
        owner = lax.rem(place[0] + step, count)
        grads[pl.ds(pl.multiple_of(owner * size, size), size), :] = piece[...]
    rows = min(QUERY_ROWS, length)
    scale = HD ** (-0.5)
    gain_total = jnp.zeros((1, HD), f32)
    for first in range(length - rows, -1, -rows):
        for head in range(queries.shape[1] // HD):
            here = (slice(first, first + rows), slice(head * HD, (head + 1) * HD))
            query, grad = queries[here], grads[here]
            log = logs[0, here[0], head : head + 1]
            parts, delta = [], 0.0
            for start, end, scores in split_scores(query, keys, first):
                probs = jnp.exp2(scores * SCORE_SCALE - log)
                prob_grad = dot(grad, values[start:end], 1, 1)
                delta += jnp.sum(probs * prob_grad, axis=1, keepdims=True)
                parts.append((start, end, probs, prob_grad))
            query_grad = 0.0
            for start, end, probs, prob_grad in parts:
                score_grad = (probs * (prob_grad - delta)).astype(bf16)
                value_part = dot(probs.astype(bf16), grad, 0, 0)
                key_part = dot(score_grad, query, 0, 0)
                query_grad += dot(score_grad, keys[start:end])
                if first + rows == length and head == 0:
                    key_grad[start:end] = key_part
                    value_grad[start:end] = value_part
                else:
                    key_grad[start:end] += key_part
                    value_grad[start:end] += value_part
            out, gain_rows = unrope_unnorm(
                query_grad * scale, q_proj[here], gains[0:1], cosine[here[0]], sine[here[0]]
            )
            q_out[here] = out.astype(bf16)
            gain_total += jnp.sum(gain_rows, axis=0, keepdims=True)
    out, gain_rows = unrope_unnorm(
        key_grad[...] * scale, k_proj[...], gains[1:2], cosine[...], sine[...]
    )
    k_out[...] = out.astype(bf16)
    v_out[...] = value_grad[...].astype(bf16)
    gain_out[0, 0:1] = gain_total
    gain_out[0, 1:2] = jnp.sum(gain_rows, axis=0, keepdims=True)


def attend_back(place, qkv, logs, pieces, saved, cosine, sine, gains, q_cols, k_cols):
    rows = qkv.shape[0]
    groups = k_cols // HD
    share = q_cols // groups
    count = len(pieces)
    return pl.pallas_call(
        lambda *refs: attend_back_kernel(count, *refs),
        out_shape=(
            jax.ShapeDtypeStruct((rows, q_cols), bf16),
            jax.ShapeDtypeStruct((rows, k_cols), bf16),
            jax.ShapeDtypeStruct((rows, k_cols), bf16),
            jax.ShapeDtypeStruct((groups, 2, HD), f32),
        ),
        grid_spec=pltpu.PrefetchScalarGridSpec(
            num_scalar_prefetch=1,
            grid=(groups,),
            in_specs=[
                pl.BlockSpec((rows, share), lambda g, p: (0, g)),
                pl.BlockSpec((rows, HD), lambda g, p: (0, q_cols // HD + g)),
                pl.BlockSpec((rows, HD), lambda g, p: (0, (q_cols + k_cols) // HD + g)),
                pl.BlockSpec((1, rows, HD), lambda g, p: (g, 0, 0)),
                pl.BlockSpec((rows, share), lambda g, p: (0, g)),
                pl.BlockSpec((rows, HD), lambda g, p: (0, q_cols // HD + g)),
                pl.BlockSpec((rows, HD), lambda g, p: (0, 0)),
                pl.BlockSpec((rows, HD), lambda g, p: (0, 0)),
                pl.BlockSpec((2, HD), lambda g, p: (0, 0)),
            ]
            + [pl.BlockSpec((rows // count, share), lambda g, p: (0, g))] * count,
            out_specs=(
                pl.BlockSpec((rows, share), lambda g, p: (0, g)),
                pl.BlockSpec((rows, HD), lambda g, p: (0, g)),
                pl.BlockSpec((rows, HD), lambda g, p: (0, g)),
                pl.BlockSpec((1, 2, HD), lambda g, p: (g, 0, 0)),
            ),
            scratch_shapes=[
                pltpu.VMEM((rows, share), bf16),
                pltpu.VMEM((rows, HD), f32),
                pltpu.VMEM((rows, HD), f32),
            ],
        ),
        compiler_params=pltpu.CompilerParams(vmem_limit_bytes=VMEM_WHOLE),
        cost_estimate=COST,
    )(place, qkv, qkv, qkv, logs, saved, saved, cosine, sine, gains, *pieces)


def normed_back_kernel(_, q_grad, k_grad, v_grad, weight, out, grads):
    @pl.when(pl.program_id(0) == 0)
    def _():
        first = 0
        for grad in (q_grad, k_grad, v_grad):
            last = first + grad.shape[1]
            grads[:, first:last] = grad[...]
            first = last

    out[...] = dot(grads[...], weight[...], 1, 1).astype(out.dtype)


def normed_back(owner, grads, weight, own_rows, dtype=f32):
    width, columns = weight.shape
    tile = min(1024, width)
    return pl.pallas_call(
        normed_back_kernel,
        out_shape=jax.ShapeDtypeStruct((own_rows, width), dtype),
        grid_spec=pltpu.PrefetchScalarGridSpec(
            num_scalar_prefetch=1,
            grid=(width // tile,),
            in_specs=[pl.BlockSpec((own_rows, g.shape[1]), lambda j, o: (o[0], 0)) for g in grads]
            + [pl.BlockSpec((tile, columns), lambda j, o: (j, 0))],
            out_specs=pl.BlockSpec((own_rows, tile), lambda j, o: (0, j)),
            scratch_shapes=[pltpu.VMEM((own_rows, columns), bf16)],
        ),
        compiler_params=pltpu.CompilerParams(vmem_limit_bytes=VMEM_WHOLE),
        cost_estimate=COST,
    )(owner, *grads, weight)


def per_device(
    tokens,
    positions,
    attn_gain,
    query_weight,
    key_weight,
    value_weight,
    query_gain,
    key_gain,
    out_weight,
    mlp_gain,
    gate_weight,
    up_weight,
    down_weight,
    cotangent,
):
    own_rows, width = tokens.shape
    count = lax.axis_size("tensor")
    place = lax.axis_index("tensor")
    assert count * own_rows == LEN
    q_cols, k_cols = query_weight.shape[1], key_weight.shape[1]
    own_width = query_weight.shape[0]
    rows_size = own_rows * width
    units = gate_weight.shape[1]
    owners = lax.rem(place - jnp.arange(count, dtype=jnp.int32) + count, count)

    x_rows = tokens.astype(f32)
    x_normal, x_scale = rms_norm(x_rows)
    digits = jnp.stack([positions // 128, positions % 128]).astype(bf16).reshape(-1)
    head_cols, out_cols = out_weight.shape
    digit_lines = -(-digits.size // (16 * out_cols)) * 16
    digits = jnp.pad(digits, (0, digit_lines * out_cols - digits.size)).reshape(-1, out_cols)
    out_lines = jnp.concatenate([out_weight, digits], axis=0)
    normed_rows = (x_normal * attn_gain).astype(bf16)
    middle = own_rows // 2
    lows, highs = [normed_rows[:middle]], [normed_rows[middle:]]

    heads_weight = after((query_weight, key_weight, value_weight), lows, highs)
    w_qkv = lax.all_gather(jnp.concatenate(heads_weight, axis=1), "dp", axis=0, tiled=True)
    out_rows = [out_lines]
    for step in range(1, count):
        pairs = [(i, (i + step) % count) for i in range(count)]
        out_rows.append(lax.ppermute(out_lines, "tensor", pairs))
    lows.append(pass_on(lows[-1], "tensor"))
    highs.append(pass_on(highs[-1], "tensor"))
    w_feed = after((gate_weight, up_weight, down_weight), out_rows[1])
    w_feed = jnp.concatenate([w_feed[0], w_feed[1], w_feed[2].T], axis=1)
    lows, highs, out_rows, w_feed = fence(lows, highs, out_rows, w_feed)
    w_out = jnp.concatenate([lines[:head_cols] for lines in out_rows], axis=0)
    w_out, w_feed = fence(w_out, w_feed)
    w_out = lax.all_gather(w_out, "dp", axis=1, tiled=True)

    group_rows = count * own_rows
    into = ()
    head_gains = jnp.stack([query_gain, key_gain])
    tables = []

    def project_block(step, into):
        digit_rows = out_rows[step][head_cols:].reshape(-1)[: 2 * own_rows]
        digit_rows = digit_rows.reshape(2, own_rows).astype(f32)
        tables.append(angle_tables(digit_rows[0] * 128.0 + digit_rows[1], HD))
        return project(
            owners[step : step + 1],
            (lows[step], highs[step]),
            w_qkv,
            *tables[-1],
            head_gains,
            into,
            group_rows,
            q_cols,
            k_cols,
        )

    for step in range(2, count):
        lows.append(pass_on(lows[-1], "tensor"))
        highs.append(pass_on(highs[-1], "tensor"))
        for block in range(0 if step == 2 else step - 1, step):
            into = project_block(block, into)
        lows[step], highs[step], into = fence(lows[step], highs[step], into)
        if step == 2:
            w_feed = lax.all_gather(after(w_feed, into), "dp", axis=0, tiled=True)
    split = own_rows * 3 // 4
    cot_low, cot_high = after((cotangent[:split], cotangent[split:]), lows[-1], highs[-1])
    cot_lows, cot_highs = [cot_low], [cot_high]
    cot_lows.append(pass_on(cot_low, "tensor"))
    into = project_block(count - 1, into)
    qkv, saved, normed = into
    cosine = in_order([pair[0] for pair in tables], "tensor", -1)
    sine = in_order([pair[1] for pair in tables], "tensor", -1)
    attended_heads, logs = attend(qkv, LEN, q_cols, k_cols)
    attended_heads, cot_lows = fence(attended_heads, cot_lows)

    pieces = [rows_of(attended_heads, place, own_rows)]
    for step in range(1, count):
        piece = rows_of(attended_heads, lax.rem(place + step, count), own_rows)
        pieces.append(lax.ppermute(piece, "tensor", [(i, (i + step) % count) for i in range(count)]))
    pieces, cot_lows, cot_highs = fence(pieces, cot_lows, cot_highs)
    attended = jnp.concatenate(pieces, axis=1)
    cot_highs.append(pass_on(cot_highs[-1], "tensor"))
    hidden_rows, mlp_rows = out_project(attended, w_out, tokens, mlp_gain)

    into = ()
    ins, parts = [mlp_rows], []
    grad_sum = mixed_sum = None
    mixed_parts = []
    for step in range(count + 2):
        if step + 1 < count:
            ins.append(pass_on(ins[-1], "tensor"))
        if step and len(cot_highs) < count:
            cot_highs.append(pass_on(cot_highs[-1], "tensor"))
        if len(cot_lows) < count:
            cot_lows.append(pass_on(cot_lows[-1], "tensor"))
        if step > 2:
            send = parts[step - 2]
            if step > 3:
                send = send + grad_sum.astype(f32)
            grad_sum = pass_on(send.astype(bf16), "tensor")
        if 2 < step <= count:
            send = mixed_parts[step - 3]
            if step > 3:
                send = send + mixed_sum.astype(f32)
            mixed_sum = pass_on(send.astype(bf16), "tensor")
        for block in {0: [], 1: [0, 1], count: [], count + 1: []}.get(step, [step]):
            into, part = feed(
                block, ins[block], (cot_lows[block], cot_highs[block]), w_feed, into, count
            )
            parts.append(part)
        if step in (1, 2) or 3 < step <= count:
            mixed_parts.append(
                down_project(step if step < 3 else step - 1, into[0], w_feed, dtype=f32)
            )
        if step == count - 1:
            gate_up_wgrad = weight_grad(into[2], into[1])
            down_wgrad = weight_grad(into[3], into[0])
            into, gate_up_wgrad, down_wgrad = fence(into, gate_up_wgrad, down_wgrad)
        ins, cot_lows, cot_highs, into, parts, grad_sum, mixed_sum, mixed_parts = fence(
            ins, cot_lows, cot_highs, into, parts, grad_sum, mixed_sum, mixed_parts
        )
        if step == count - 1:
            gate_up_wgrad = after(gate_up_wgrad, into)
            gate_up_sum = lax.psum_scatter(gate_up_wgrad, "dp", scatter_dimension=0, tiled=True)

    send = (mixed_parts[-1] + mixed_sum.astype(f32)).astype(bf16)
    last_low = pass_on(send[:middle], "tensor")
    rows_grad, branch_grad, mlp_gain_part, pieces = out_back(
        count, parts[0], grad_sum, cotangent, hidden_rows, mlp_gain, w_out
    )
    pieces, branch_grad, last_low, send = fence(pieces, branch_grad, last_low, send)

    for step in range(1, count):
        pieces[step] = lax.ppermute(
            pieces[step], "tensor", [(i, (i - step) % count) for i in range(count)]
        )
    out_wgrad = weight_grad(branch_grad, attended)
    pieces, out_wgrad, send = fence(pieces, out_wgrad, send)
    out_block = lax.psum_scatter(out_wgrad, "dp", scatter_dimension=0, tiled=True)

    last_high = pass_on(send[middle:], "tensor")
    *head_grads, gain_parts = attend_back(
        place.reshape(1),
        qkv,
        logs,
        pieces,
        saved,
        cosine,
        sine,
        head_gains,
        q_cols,
        k_cols,
    )
    head_grads, gain_parts, last_high = fence(head_grads, gain_parts, last_high)
    mixed_sum = jnp.concatenate([last_low, last_high], axis=0)
    first_part = normed_back(owners[1:2], head_grads, w_qkv, own_rows, bf16)
    normed_sum = pass_on(first_part, "tensor")

    head_grads = after(head_grads, first_part)
    part = normed_back(owners[2 % count :][:1], head_grads, w_qkv, own_rows)
    qkv_wgrad, attn_gain_part = head_weight_grad(normed, head_grads, w_qkv)
    gains = jnp.concatenate(
        [
            jnp.sum(attn_gain_part, axis=1) / attn_gain,
            mlp_gain_part,
            jnp.sum(gain_parts, axis=0).reshape(-1),
        ]
    )
    beside_cols = -(-gains.size // (own_width // 2 * HD)) * HD
    beside = jnp.pad(gains, (0, own_width * beside_cols - gains.size))
    beside = beside.reshape(own_width, beside_cols).astype(bf16)
    qkv_sum = HalvingSum(qkv_wgrad, "dp", beside).prepare().launch(rows_size // 2)
    normed_sum, part, qkv_sum.state, gate_up_sum = fence(
        normed_sum, part, qkv_sum.state, gate_up_sum
    )
    down_wgrad = after(down_wgrad, normed_sum)
    down_sum = lax.psum_scatter(down_wgrad, "dp", scatter_dimension=0, tiled=True)
    out_pieces = []
    for step in range(2, count):
        send = (part + normed_sum.astype(f32)).astype(bf16)
        normed_sum = pass_on(send, "tensor")
        qkv_sum.state, head_grads = fence(qkv_sum.state, head_grads, send)[:2]
        if qkv_sum.steps < qkv_sum.bits:
            qkv_sum.prepare().launch(rows_size)
        if step == 2:
            mixed = down_project(0, into[0], w_feed, mixed_sum, hidden_rows)
        if step == count - 1:
            out_block = after(out_block, send)
            out_pieces = [out_block[:, s * head_cols : (s + 1) * head_cols] for s in range(count)]
            gate_sum = gate_up_sum[:, :units].astype(f32)
            up_sum = gate_up_sum[:, units:].astype(f32)
        part = normed_back(owners[(step + 1) % count :][:1], head_grads, w_qkv, own_rows)
        if step == count - 1:
            qkv_total = qkv_sum.total(f32)
            normed_sum, part, qkv_total, out_pieces, mixed = fence(
                normed_sum, part, qkv_total, out_pieces, mixed
            )
        else:
            normed_sum, part, qkv_sum.state, out_pieces, mixed = fence(
                normed_sum, part, qkv_sum.state, out_pieces, mixed
            )

    for other in range(1, count):
        pairs = [(i, (i - other) % count) for i in range(count)]
        out_pieces[other] = lax.ppermute(out_pieces[other], "tensor", pairs)
    out_total = sum(piece.astype(f32) for piece in out_pieces).T
    gains = qkv_total[:, q_cols + 2 * k_cols :].reshape(-1)[: gains.size]
    gains = after(gains.reshape(-1, HD), out_pieces[1])
    gains = butterfly_sum(gains, "tensor").reshape(-1)
    normed_grad = part + normed_sum.astype(f32)
    token_grad = (rows_grad + rms_back(normed_grad, attn_gain, x_normal, x_scale)).astype(bf16)
    return (
        mixed,
        token_grad,
        gains[:width],
        qkv_total[:, :q_cols],
        qkv_total[:, q_cols : q_cols + k_cols],
        qkv_total[:, q_cols + k_cols : q_cols + 2 * k_cols],
        gains[2 * width : 2 * width + HD],
        gains[2 * width + HD : 2 * width + 2 * HD],
        out_total,
        gains[width : 2 * width],
        gate_sum,
        up_sum,
        down_sum.astype(f32).T,
    )


def solution(mesh):
    in_specs = (
        P(("dp", "tensor"), None),
        P(("dp", "tensor")),
        P(),
        P("dp", "tensor"),
        P("dp", "tensor"),
        P("dp", "tensor"),
        P(),
        P(),
        P("tensor", "dp"),
        P(),
        P("dp", "tensor"),
        P("dp", "tensor"),
        P("tensor", "dp"),
        P(("dp", "tensor"), None),
    )
    out_specs = (
        P(("dp", "tensor"), None),
        P(("dp", "tensor"), None),
        P(),
        P("dp", "tensor"),
        P("dp", "tensor"),
        P("dp", "tensor"),
        P(),
        P(),
        P("tensor", "dp"),
        P(),
        P("dp", "tensor"),
        P("dp", "tensor"),
        P("tensor", "dp"),
    )
    return jax.shard_map(
        per_device, mesh=mesh, in_specs=in_specs, out_specs=out_specs, check_vma=False
    )
```
